32 devices in a mesh: vox: 8 (over z, y), comp: 4 (over x, core).
Axes of the slice: x: 2, y: 2, z: 4, core: 2. Of those that a mesh axis runs over, the one named last changes fastest.
Arguments:
- data: bfloat16 [2048, 8192], P('comp', 'vox'), may hold values from -108 to 108
- projection: bfloat16 [512, 2048], P(None, 'comp'), may hold values from -0.125 to 0.125
- initial: float32 [512, 512], P('comp'), may hold values from -0.25 to 0.25
Outputs:
- unmixing: float32 [512, 512], P('comp')
- sources: bfloat16 [512, 8192], P('comp', 'vox')
The draws below stay inside these ranges and needn't reach their ends.
All inputs are finite; a program needn't handle non-finite values.
Results may differ from the reference program's by a relative error of at most 0.008.
Values may be sent and summed in bfloat16 or wider, within the bound.
No kernel may reach another device: no remote copies, remote signals or barrier semaphores. Data moves between devices by JAX's collectives and lax.ppermute only.
A program may use at most 64 MiB of HBM per device.

```python
import math
import jax
import jax.numpy as jnp
from jax import lax

P_SIZE = 2048
K = 512
ICA_ITERS = 2
WHITEN_STEPS = 3
DECOR_STEPS = 3
VOXELS = 8192


def draw_data(key, part):
    key_base = jax.random.fold_in(key, 11)
    key_rows = jax.random.fold_in(key, 12)
    key_cols = jax.random.fold_in(key, 13)
    base = jnp.clip(jax.random.normal(key_base, (P_SIZE, VOXELS), jnp.float32), -6.0, 6.0)
    rows = jnp.exp(jax.random.uniform(key_rows, (P_SIZE, 1), jnp.float32, math.log(0.5), math.log(2.0)))
    cols = jnp.exp(jax.random.uniform(key_cols, (1, VOXELS), jnp.float32, math.log(0.3), math.log(3.0)))
    place = jnp.arange(VOXELS, dtype=jnp.float32)[None, :] / (VOXELS - 1)
    trend = jnp.exp(math.log(3.0) * place)
    return (base * rows * cols * trend).astype(jnp.bfloat16)


def block_levels(stream_key, extent, shards, smallest, top_value):
    gain, own = 1.0, jax.random.fold_in(stream_key, 6)
    for position, parts in shards:
        steps = jnp.exp(jax.random.uniform(jax.random.fold_in(own, position), (parts,), jnp.float32, smallest / len(shards), top_value / len(shards)))
        gain = gain * jnp.repeat(steps, extent[position] // parts).reshape([-1 if axis == position else 1 for axis in range(len(extent))])
    return gain


def centred(own_key, extent, scale, limit, shards=(), kind=jnp.bfloat16):
    gain = block_levels(own_key, extent, shards, -0.22, 0.18) if shards else 1.0
    entries = jax.random.normal(own_key, extent, jnp.float32) * scale * gain
    return jnp.minimum(jnp.maximum(entries, -limit), limit).astype(kind)


def setup_inputs(seed: int = 0) -> dict:
    seeds = jax.random.split(jax.random.key(seed), 4)
    data = draw_data(jax.random.fold_in(seeds[3], 71), 0)
    projection = centred(seeds[1], (K, P_SIZE), P_SIZE ** -0.5, 0.125, ((1, 4),))
    initial = centred(seeds[2], (K, K), K ** -0.5, 0.25, ((0, 4),), jnp.float32)
    return {"data": data, "projection": projection, "initial": initial}


def mult(left, right):
    return jnp.dot(left, right, precision=lax.Precision.HIGHEST)

def whitening(covar):
    count = covar.shape[0]
    eye = jnp.eye(count, dtype=jnp.float32)
    cscale = jnp.sqrt(jnp.sum(covar * covar) + 1e-06)
    ymat = covar / cscale
    zmat = eye
    for step in range(WHITEN_STEPS):
        middle = 1.5 * eye - 0.5 * mult(zmat, ymat)
        ymat = mult(ymat, middle)
        zmat = mult(middle, zmat)
    return (zmat / jnp.sqrt(cscale)).astype(jnp.bfloat16)

def decorrelate(newer):
    gram = mult(newer, newer.T)
    newer = newer / jnp.sqrt(jnp.sqrt(jnp.sum(gram * gram) + 1e-06))
    for step in range(DECOR_STEPS):
        newer = 1.5 * newer - 0.5 * mult(mult(newer, newer.T), newer)
    return newer

def reference(data, projection, initial):
    reduced = jnp.dot(projection, data, preferred_element_type=jnp.float32).astype(jnp.bfloat16)
    covar = jnp.dot(reduced, reduced.T, preferred_element_type=jnp.float32) / VOXELS
    whiten = whitening(covar)
    whitened = jnp.dot(whiten, reduced, preferred_element_type=jnp.float32).astype(jnp.bfloat16)
    unmixing = initial
    for turn in range(ICA_ITERS):
        scores = jnp.dot(unmixing.astype(jnp.bfloat16), whitened, preferred_element_type=jnp.float32)
        bent = jnp.tanh(scores)
        pulled = jnp.dot(bent.astype(jnp.bfloat16), whitened.T, preferred_element_type=jnp.float32)
        slope = lax.optimization_barrier(jnp.sum(1.0 - bent * bent, axis=1))
        newer = pulled - slope[:, None] * unmixing
        unmixing = decorrelate(newer)
    sources = jnp.dot(unmixing.astype(jnp.bfloat16), whitened, preferred_element_type=jnp.float32).astype(jnp.bfloat16)
    return (unmixing, sources)
```

```python
import jax
import jax.numpy as jnp
from jax import lax
from jax.sharding import PartitionSpec as P

ICA_ITERS = 2
AXES = ("vox", "comp")
BF = jnp.bfloat16
F32 = jnp.float32


def mult(left, right):
    return jnp.dot(left, right, precision=lax.Precision.HIGH)


def mult_t(left, right):
    return lax.dot_general(
        left, right, (((1,), (1,)), ((), ())), precision=lax.Precision.HIGH
    )


def dot(left, right, dims):
    return lax.dot_general(left, right, (dims, ((), ())), preferred_element_type=F32)


def flip(x, mask):
    count = lax.axis_size("vox") * lax.axis_size("comp")
    return lax.ppermute(x, AXES, [(i, i ^ mask) for i in range(count)])


def pairs(masks):
    return [masks[i : i + 2] for i in range(0, len(masks), 2)]


def sum_over(x, masks):
    for group in pairs(masks):
        sent = x.astype(BF)
        x = sent.astype(F32) + flip(sent, group[0]).astype(F32)
        if len(group) == 2:
            x = x + (
                flip(sent, group[1]).astype(F32)
                + flip(sent, group[0] | group[1]).astype(F32)
            )
    return x


def place(x, other, bit):
    first = jnp.where(bit == 0, x, other)
    second = jnp.where(bit == 0, other, x)
    return jnp.stack([first, second])


def whitening(covar):
    cscale = jnp.sqrt(jnp.sum(covar * covar) + 1e-06)
    y = covar / cscale
    eye = jnp.eye(y.shape[0], dtype=F32)
    square = mult(y, y)
    z2 = 2.25 * eye - 2.4375 * y + mult(
        square, 1.6875 * eye - 0.5625 * y + 0.0625 * square
    )
    z3 = 1.5 * z2 - 0.5 * mult(mult(y, z2), mult(z2, z2))
    return (z3 / jnp.sqrt(cscale)).astype(BF)


def decorrelate(newer):
    gram = mult_t(newer, newer)
    gscale = jnp.sqrt(jnp.sum(gram * gram) + 1e-06)
    newer = newer / jnp.sqrt(gscale)
    newer = 1.5 * newer - 0.5 * mult(gram / gscale, newer)
    for step in range(2):
        newer = 1.5 * newer - 0.5 * mult(mult_t(newer, newer), newer)
    return newer


def shards(data, projection, initial):
    comps = lax.axis_size("comp")
    voxels = data.shape[1] * lax.axis_size("vox")
    vox, comp = lax.axis_index("vox"), lax.axis_index("comp")
    index = vox * comps + comp
    comp_bits = comps.bit_length() - 1
    all_bits = (lax.axis_size("vox") * comps).bit_length() - 1
    low, across, near = 1, 2, comps
    far = [1 << k for k in range(comp_bits + 1, all_bits)]

    def bit(mask):
        return jnp.where((index & mask) == 0, 0, 1)

    def pick(x, axis, which):
        return lax.dynamic_index_in_dim(x, which, axis, keepdims=False)

    part = dot(data, projection, ((0,), (1,)))
    rows = part.shape[1]
    part = part.reshape((2, 2, part.shape[0] // 4, rows))
    sent = flip(pick(part, 1, 1 - bit(low)).astype(BF), low)
    part = pick(part, 1, bit(low)) + sent.astype(F32)
    sent = flip(pick(part, 0, 1 - bit(across)).astype(BF), across)
    reduced = (pick(part, 0, bit(across)) + sent.astype(F32)).astype(BF)

    size = comps * 2
    groups = [list(range(g * size, (g + 1) * size)) for g in range((1 << all_bits) // size)]
    gathered = lax.all_gather(reduced, AXES, axis=0, tiled=True, axis_index_groups=groups)

    both = jnp.concatenate([reduced, flip(reduced, low)])
    half = rows // 2
    mine = lax.dynamic_slice_in_dim(both, bit(low) * half, half, 1)
    covar = dot(mine, both, ((0,), (0,))).reshape(2, 2, half // 4, rows)
    bx, by = bit(across), bit(near)

    def quarter(i, j):
        return pick(pick(covar, 0, i), 0, j)

    total = quarter(bx, by) + flip(quarter(1 - bx, by).astype(BF), across).astype(F32)
    total = total + flip(quarter(bx, 1 - by).astype(BF), near).astype(F32)
    total = total + flip(quarter(1 - bx, 1 - by).astype(BF), across | near).astype(F32)
    total = sum_over(total, far).astype(BF)

    def spread(x):
        here = place(x, flip(x, near), by)
        there = place(flip(x, across), flip(x, across | near), by)
        return place(here, there, bx)

    total = spread(total).reshape(half, rows)
    covar = place(total, flip(total, low), bit(low)).reshape(rows, rows)
    whiten = whitening(covar.astype(F32) / voxels)
    whitened = dot(gathered, whiten, ((1,), (1,))).astype(BF)

    count = initial.shape[0] // 2
    weights = lax.dynamic_slice_in_dim(initial, by * count, count, 0)
    for turn in range(ICA_ITERS):
        scores = dot(weights.astype(BF), whitened, ((1,), (1,)))
        bent = jnp.tanh(scores)
        pulled = dot(bent.astype(BF), whitened, ((1,), (0,)))
        slope = jnp.sum(1.0 - bent * bent, axis=1)
        newer = pulled - slope[:, None] * weights
        newer = spread(sum_over(newer, far).astype(BF))
        newer = newer.reshape((2, 2 * count, rows))
        newer = jnp.swapaxes(place(newer, flip(newer, low), bit(low)), 0, 1)
        whole = decorrelate(newer.reshape(rows, rows).astype(F32))
        mine = lax.dynamic_slice_in_dim(whole, comp * 2 * count, 2 * count, 0)
        weights = lax.dynamic_slice_in_dim(mine, by * count, count, 0)
    own = lax.dynamic_slice_in_dim(whitened, by * data.shape[1], data.shape[1], 0)
    sources = dot(mine.astype(BF), own, ((1,), (1,))).astype(BF)
    return (mine, sources)


def solution(mesh):
    return jax.shard_map(
        shards,
        mesh=mesh,
        in_specs=(P("comp", "vox"), P(None, "comp"), P("comp", None)),
        out_specs=(P("comp", None), P("comp", "vox")),
        check_vma=False,
    )
```

```python
import functools

import jax
import jax.numpy as jnp
from jax import lax
from jax.experimental import pallas as pl
from jax.experimental.pallas import tpu as pltpu
from jax.sharding import PartitionSpec as P

ICA_ITERS = 2
AXES = ("vox", "comp")
BF = jnp.bfloat16
F32 = jnp.float32
MIB = 1 << 20


def nn(left, right):
    return jnp.dot(left, right, preferred_element_type=F32)


def nt(left, right):
    return lax.dot_general(
        left, right, (((1,), (1,)), ((), ())), preferred_element_type=F32
    )


def rounded(x):
    return lax.reduce_precision(x, 8, 7)


def flip(x, mask):
    count = lax.axis_size("vox") * lax.axis_size("comp")
    return lax.ppermute(x, AXES, [(i, i ^ mask) for i in range(count)])


def sum_over(x, masks):
    for k in range(0, len(masks), 2):
        sent = x.astype(BF)
        x = rounded(x) + flip(sent, masks[k]).astype(F32)
        if k + 1 < len(masks):
            x = x + (
                flip(sent, masks[k + 1]).astype(F32)
                + flip(sent, masks[k] | masks[k + 1]).astype(F32)
            )
    return x


def spread(x, across, near):
    return jnp.stack([x, flip(x, near), flip(x, across), flip(x, across | near)])


VMEM = pl.BlockSpec(memory_space=pltpu.VMEM)
SMEM = pl.BlockSpec(memory_space=pltpu.SMEM)
ANY = pl.BlockSpec(memory_space=pl.ANY)


def run(kernel, outs, args, specs=None, scratch=(), limit=24):
    return pl.pallas_call(
        kernel,
        out_shape=outs,
        in_specs=specs or [SMEM] + [VMEM] * (len(args) - 1),
        out_specs=jax.tree.map(lambda _: VMEM, outs),
        scratch_shapes=list(scratch),
        compiler_params=pltpu.CompilerParams(vmem_limit_bytes=limit * MIB),
    )(*args)


def shape(dims, dtype):
    return jax.ShapeDtypeStruct(dims, dtype)


def project_kernel(away, at, left_ref, right_ref, other_left_ref, other_right_ref, out_ref):
    size = other_right_ref.shape[1]
    across = 1 - at[1] if away else at[1]
    start = pl.multiple_of((across * 2 + at[0]) * size, size)
    total = nn(left_ref[...], right_ref[:, pl.ds(start, size)])
    total += nn(other_left_ref[...], other_right_ref[...])
    out_ref[...] = total.astype(out_ref.dtype)


def covar_kernel(at, here_ref, there_ref, own_ref, y_ref, x_ref, xy_ref, both, pack):
    rows, size = here_ref.shape
    block = rows // 4
    both[:, :size] = here_ref[...]
    both[:, size:] = there_ref[...]

    def part(k):
        return both[pl.ds(pl.multiple_of(k * block, block), block), :]

    low = at[0]
    first, second = part(2 * low), part(2 * low + 1)
    third = part(2 - 2 * low)
    pack[0 * block : 1 * block] = nt(first, first)
    pack[1 * block : 2 * block] = nt(first, second)
    pack[2 * block : 3 * block] = nt(second, second)
    pack[3 * block : 4 * block] = nt(second, third)
    pack[4 * block : 5 * block] = nt(part(low), part(2 + low))
    piece = own_ref.shape[0]

    def quarter(i, j):
        return pack[pl.ds(pl.multiple_of((2 * i + j) * piece, piece), piece), :]

    ax, ay = at[1], at[2]
    own_ref[...] = quarter(ax, ay)
    y_ref[...] = quarter(ax, 1 - ay).astype(BF)
    x_ref[...] = quarter(1 - ax, ay).astype(BF)
    xy_ref[...] = quarter(1 - ax, 1 - ay).astype(BF)


def whiten_kernel(voxels, at, mine_ref, other_ref, out_ref, packs, covar):
    piece = mine_ref.shape[1]
    block = mine_ref.shape[2]
    rows = covar.shape[0]
    low, ax, ay = at[0], at[1], at[2]
    for k in range(4):
        i, j = ax ^ (k >> 1), ay ^ (k & 1)
        place = pl.ds(pl.multiple_of((2 * i + j) * piece, piece), piece)
        packs[low, place, :] = mine_ref[k].astype(F32)
        packs[1 - low, place, :] = other_ref[k].astype(F32)

    def put(i, j, core, k):
        value = packs[core, k * block : (k + 1) * block, :]
        covar[i * block : (i + 1) * block, j * block : (j + 1) * block] = value
        if i != j:
            covar[j * block : (j + 1) * block, i * block : (i + 1) * block] = value.T

    for core in (0, 1):
        a, b, c = 2 * core, 2 * core + 1, 2 - 2 * core
        put(a, a, core, 0)
        put(a, b, core, 1)
        put(b, b, core, 2)
        put(b, c, core, 3)
        put(core, 2 + core, core, 4)

    y = covar[...] / voxels
    cscale = jnp.sqrt(jnp.sum(y * y) + 1e-06)
    y = y / cscale
    eye = (
        lax.broadcasted_iota(jnp.int32, (rows, rows), 0)
        == lax.broadcasted_iota(jnp.int32, (rows, rows), 1)
    ).astype(F32)
    yb = y.astype(BF)
    square = nn(yb, yb)
    squared = square.astype(BF)
    rest = -2.4375 * y + 1.6875 * square
    rest += nn(squared, (0.0625 * square - 0.5625 * y).astype(BF))
    restb = rest.astype(BF)
    left = 2.25 * y + nn(yb, restb)
    right = 4.5 * rest + nn(restb, restb)
    z3 = 3.375 * eye + 1.5 * rest - 0.5 * (
        5.0625 * left + nn(left.astype(BF), right.astype(BF))
    )
    out_ref[...] = (z3 / jnp.sqrt(cscale)).astype(BF)


def step(weights, block):
    bent = jnp.tanh(nn(weights.astype(BF), block))
    pulled = nt(bent.astype(BF), block)
    return pulled, jnp.sum(1.0 - bent * bent, axis=1, keepdims=True)


def apply_kernel(whiten_ref, block_ref, weights_ref, white_ref, newer_ref, total, slope):
    turn = pl.program_id(0)

    @pl.when(turn == 0)
    def _():
        total[...] = jnp.zeros_like(total)
        slope[...] = jnp.zeros_like(slope)

    weights = weights_ref[...]
    for k in range(block_ref.shape[0]):
        white = nn(whiten_ref[...], block_ref[k]).astype(BF)
        white_ref[k] = white
        pulled, part = step(weights, white)
        total[...] += pulled
        slope[...] += part

    @pl.when(turn == pl.num_programs(0) - 1)
    def _():
        newer_ref[...] = total[...] - slope[...] * weights


def decor_kernel(last, at, mine_ref, other_ref, white_ref, *refs):
    outs, (newer, lower, white, sem) = refs[:-4], refs[-4:]
    count = mine_ref.shape[1]
    low, ax, ay = at[0], at[1], at[2]
    chunks = white.shape[0]
    source = white_ref.at[pl.ds(ay * chunks, chunks)] if last else white_ref
    copy = pltpu.make_async_copy(source, white, sem)
    copy.start()
    for k in range(4):
        i, j = ax ^ (k >> 1), ay ^ (k & 1)
        for ref, core in ((mine_ref, low), (other_ref, 1 - low)):
            start = pl.multiple_of((4 * i + 2 * core + j) * count, count)
            lower[pl.ds(start, count), :] = ref[k]

    raw = lower[...]
    gram = nt(raw, raw)
    gscale = jnp.sqrt(jnp.sum(gram * gram) + 1e-06)
    gram = (gram / gscale).astype(BF)
    value = (1.5 * raw.astype(F32) - 0.5 * nn(gram, raw)) / jnp.sqrt(gscale)
    raw = value.astype(BF)
    gram = nt(raw, raw).astype(BF)
    newer[...] = 1.5 * value - 0.5 * nn(gram, raw)
    lower[...] = newer[...].astype(BF)
    start = pl.multiple_of((4 * ax + 2 * low) * count, count)
    size = 2 * count
    if not last:
        start = pl.multiple_of(start + ay * count, count)
        size = count
    raw = lower[...]
    gram = nt(lower[pl.ds(start, size), :], raw).astype(BF)
    weights = 1.5 * newer[pl.ds(start, size), :] - 0.5 * nn(gram, raw)
    copy.wait()
    if last:
        outs[0][...] = weights
        width = white.shape[2]
        for k in range(chunks):
            outs[1][:, k * width : (k + 1) * width] = nn(
                weights.astype(BF), white[k]
            ).astype(BF)
    else:
        total, slope = step(weights, white[0])
        for k in range(1, chunks):
            pulled, part = step(weights, white[k])
            total += pulled
            slope += part
        outs[0][...] = total - slope * weights


def shards(data, projection, initial):
    comps = lax.axis_size("comp")
    voxels = data.shape[1] * lax.axis_size("vox")
    vox, comp = lax.axis_index("vox"), lax.axis_index("comp")
    index = vox * comps + comp
    all_bits = (lax.axis_size("vox") * comps).bit_length() - 1
    low, across, near = 1, 2, comps
    far = [1 << k for k in range(near.bit_length(), all_bits)]
    at = jnp.stack([comp & 1, comp >> 1, vox & 1]).astype(jnp.int32)
    rows = projection.shape[0]
    size = data.shape[1] // comps

    def columns(x):
        start = (x * 2 + (1 - at[0])) * size
        return flip(lax.dynamic_slice_in_dim(data, start, size, 1), low)

    other = flip(projection, low)
    sent = run(
        functools.partial(project_kernel, True),
        shape((rows, size), BF),
        (at, projection, data, other, columns(1 - at[1])),
    )
    kept = run(
        functools.partial(project_kernel, False),
        shape((rows, size), F32),
        (at, projection, data, other, columns(at[1])),
    )
    reduced = (kept + flip(sent, across).astype(F32)).astype(BF)

    near_size = comps * 2
    groups = [
        list(range(g, g + near_size)) for g in range(0, 1 << all_bits, near_size)
    ]
    gathered = lax.all_gather(reduced, AXES, axis=0, axis_index_groups=groups)

    block = rows // 4
    piece = 5 * block // 4
    small = shape((piece, block), BF)
    own, by, bx, bxy = run(
        covar_kernel,
        (shape((piece, block), F32), small, small, small),
        (at, reduced, flip(reduced, low)),
        scratch=[pltpu.VMEM((rows, 2 * size), BF), pltpu.VMEM((5 * block, block), F32)],
    )
    own = own + flip(by, near).astype(F32)
    own = own + flip(bx, across).astype(F32)
    own = own + flip(bxy, across | near).astype(F32)
    packed = spread(sum_over(own, far).astype(BF), across, near)
    whiten = run(
        functools.partial(whiten_kernel, voxels),
        shape((rows, rows), BF),
        (at, packed, flip(packed, low)),
        scratch=[pltpu.VMEM((2, 5 * block, block), F32), pltpu.VMEM((rows, rows), F32)],
    )

    count = initial.shape[0] // 2
    weights = lax.dynamic_slice_in_dim(initial, at[2] * count, count, 0)
    steps = 4
    per = near_size // steps
    whitened, newer = pl.pallas_call(
        apply_kernel,
        grid=(steps,),
        out_shape=(shape((near_size, rows, size), BF), shape((count, rows), F32)),
        in_specs=[
            pl.BlockSpec((rows, rows), lambda i: (0, 0)),
            pl.BlockSpec((per, rows, size), lambda i: (i, 0, 0)),
            pl.BlockSpec((count, rows), lambda i: (0, 0)),
        ],
        out_specs=(
            pl.BlockSpec((per, rows, size), lambda i: (i, 0, 0)),
            pl.BlockSpec((count, rows), lambda i: (0, 0)),
        ),
        scratch_shapes=[pltpu.VMEM((count, rows), F32), pltpu.VMEM((count, 1), F32)],
        compiler_params=pltpu.CompilerParams(vmem_limit_bytes=24 * MIB),
    )(whiten, gathered, weights)

    for turn in range(ICA_ITERS):
        last = turn == ICA_ITERS - 1
        stacked = spread(sum_over(newer, far).astype(BF), across, near)
        chunks = comps if last else near_size
        outs = (
            (shape((2 * count, rows), F32), shape((2 * count, data.shape[1]), BF))
            if last
            else shape((count, rows), F32)
        )
        newer = run(
            functools.partial(decor_kernel, last),
            outs,
            (at, stacked, flip(stacked, low), whitened),
            specs=[SMEM, VMEM, VMEM, ANY],
            scratch=[
                pltpu.VMEM((rows, rows), F32),
                pltpu.VMEM((rows, rows), BF),
                pltpu.VMEM((chunks, rows, size), BF),
                pltpu.SemaphoreType.DMA,
            ],
        )
    return newer


def solution(mesh):
    return jax.shard_map(
        shards,
        mesh=mesh,
        in_specs=(P("comp", "vox"), P(None, "comp"), P("comp", None)),
        out_specs=(P("comp", None), P("comp", "vox")),
        check_vma=False,
    )
```

```python
import functools

import jax
import jax.numpy as jnp
from jax import lax
from jax.experimental import pallas as pl
from jax.experimental.pallas import tpu as pltpu
from jax.sharding import PartitionSpec as P

ICA_ITERS = 2
AXES = ("vox", "comp")
BF = jnp.bfloat16
F32 = jnp.float32
MIB = 1 << 20


def nn(left, right):
    return jnp.dot(left, right, preferred_element_type=F32)


def nt(left, right):
    return lax.dot_general(
        left, right, (((1,), (1,)), ((), ())), preferred_element_type=F32
    )


def rounded(x):
    return lax.reduce_precision(x, 8, 7)


def flip(x, mask):
    count = lax.axis_size("vox") * lax.axis_size("comp")
    return lax.ppermute(x, AXES, [(i, i ^ mask) for i in range(count)])


def sum_over(x, masks):
    for k in range(0, len(masks), 2):
        sent = x.astype(BF)
        x = rounded(x) + flip(sent, masks[k]).astype(F32)
        if k + 1 < len(masks):
            x = x + (
                flip(sent, masks[k + 1]).astype(F32)
                + flip(sent, masks[k] | masks[k + 1]).astype(F32)
            )
    return x


def spread(x, across, near):
    return jnp.stack([x, flip(x, near), flip(x, across), flip(x, across | near)])


VMEM = pl.BlockSpec(memory_space=pltpu.VMEM)
SMEM = pl.BlockSpec(memory_space=pltpu.SMEM)
ANY = pl.BlockSpec(memory_space=pl.ANY)


def run(kernel, outs, args, specs=None, scratch=(), limit=24):
    return pl.pallas_call(
        kernel,
        out_shape=outs,
        in_specs=specs or [SMEM] + [VMEM] * (len(args) - 1),
        out_specs=jax.tree.map(lambda _: VMEM, outs),
        scratch_shapes=list(scratch),
        compiler_params=pltpu.CompilerParams(vmem_limit_bytes=limit * MIB),
    )(*args)


def shape(dims, dtype):
    return jax.ShapeDtypeStruct(dims, dtype)


def project_kernel(away, at, left_ref, right_ref, other_left_ref, other_right_ref, out_ref):
    size = other_right_ref.shape[1]
    across = 1 - at[1] if away else at[1]
    start = pl.multiple_of((across * 2 + at[0]) * size, size)
    total = nn(left_ref[...], right_ref[:, pl.ds(start, size)])
    total += nn(other_left_ref[...], other_right_ref[...])
    out_ref[...] = total.astype(out_ref.dtype)


def covar_kernel(at, here_ref, there_ref, own_ref, y_ref, x_ref, xy_ref, both, pack):
    rows, size = here_ref.shape
    block = rows // 4
    both[:, :size] = here_ref[...]
    both[:, size:] = there_ref[...]

    def part(k):
        return both[pl.ds(pl.multiple_of(k * block, block), block), :]

    low = at[0]
    first, second = part(2 * low), part(2 * low + 1)
    third = part(2 - 2 * low)
    pack[0 * block : 1 * block] = nt(first, first)
    pack[1 * block : 2 * block] = nt(first, second)
    pack[2 * block : 3 * block] = nt(second, second)
    pack[3 * block : 4 * block] = nt(second, third)
    pack[4 * block : 5 * block] = nt(part(low), part(2 + low))
    piece = own_ref.shape[0]

    def quarter(i, j):
        return pack[pl.ds(pl.multiple_of((2 * i + j) * piece, piece), piece), :]

    ax, ay = at[1], at[2]
    own_ref[...] = quarter(ax, ay)
    y_ref[...] = quarter(ax, 1 - ay).astype(BF)
    x_ref[...] = quarter(1 - ax, ay).astype(BF)
    xy_ref[...] = quarter(1 - ax, 1 - ay).astype(BF)


def whiten_kernel(voxels, at, mine_ref, other_ref, out_ref, packs, covar):
    piece = mine_ref.shape[1]
    block = mine_ref.shape[2]
    rows = covar.shape[0]
    low, ax, ay = at[0], at[1], at[2]
    for k in range(4):
        i, j = ax ^ (k >> 1), ay ^ (k & 1)
        place = pl.ds(pl.multiple_of((2 * i + j) * piece, piece), piece)
        packs[low, place, :] = mine_ref[k].astype(F32)
        packs[1 - low, place, :] = other_ref[k].astype(F32)

    def put(i, j, core, k):
        value = packs[core, k * block : (k + 1) * block, :]
        covar[i * block : (i + 1) * block, j * block : (j + 1) * block] = value
        if i != j:
            covar[j * block : (j + 1) * block, i * block : (i + 1) * block] = value.T

    for core in (0, 1):
        a, b, c = 2 * core, 2 * core + 1, 2 - 2 * core
        put(a, a, core, 0)
        put(a, b, core, 1)
        put(b, b, core, 2)
        put(b, c, core, 3)
        put(core, 2 + core, core, 4)

    y = covar[...] / voxels
    cscale = jnp.sqrt(jnp.sum(y * y) + 1e-06)
    y = y / cscale
    eye = (
        lax.broadcasted_iota(jnp.int32, (rows, rows), 0)
        == lax.broadcasted_iota(jnp.int32, (rows, rows), 1)
    ).astype(F32)
    yb = y.astype(BF)
    square = nn(yb, yb)
    squared = square.astype(BF)
    rest = -2.4375 * y + 1.6875 * square
    rest += nn(squared, (0.0625 * square - 0.5625 * y).astype(BF))
    restb = rest.astype(BF)
    left = 2.25 * y + nn(yb, restb)
    right = 4.5 * rest + nn(restb, restb)
    z3 = 3.375 * eye + 1.5 * rest - 0.5 * (
        5.0625 * left + nn(left.astype(BF), right.astype(BF))
    )
    out_ref[...] = (z3 / jnp.sqrt(cscale)).astype(BF)


def step(weights, block):
    bent = jnp.tanh(nn(weights.astype(BF), block))
    pulled = nt(bent.astype(BF), block)
    return pulled, jnp.sum(1.0 - bent * bent, axis=1, keepdims=True)


def apply_kernel(part, whiten_ref, *refs):
    blocks, (weights_ref, white_ref, total_ref, slope_ref) = refs[:4], refs[-4:]
    weights = weights_ref[...]
    total, slope = refs[4][...] if part else 0.0, refs[5][...] if part else 0.0
    for k in range(4):
        white = nn(whiten_ref[...], blocks[k][...]).astype(BF)
        white_ref[k] = white
        pulled, sums = step(weights, white)
        total += pulled
        slope += sums
    if part:
        total -= slope * weights
    total_ref[...] = total
    slope_ref[...] = slope


def decor_kernel(last, at, mine_ref, other_ref, *refs):
    sources = 1 if last else 2
    whites, outs, (newer, lower, white, sem) = refs[:sources], refs[sources:-4], refs[-4:]
    count = mine_ref.shape[1]
    low, ax, ay = at[0], at[1], at[2]
    chunks = white.shape[0]
    copies = [
        pltpu.make_async_copy(ref, white.at[pl.ds(4 * k, 4)], sem.at[k])
        for k, ref in enumerate(whites)
    ]
    for copy in copies:
        copy.start()
    for k in range(4):
        i, j = ax ^ (k >> 1), ay ^ (k & 1)
        for ref, core in ((mine_ref, low), (other_ref, 1 - low)):
            start = pl.multiple_of((4 * i + 2 * core + j) * count, count)
            lower[pl.ds(start, count), :] = ref[k]

    raw = lower[...]
    gram = nt(raw, raw)
    gscale = jnp.sqrt(jnp.sum(gram * gram) + 1e-06)
    gram = (gram / gscale).astype(BF)
    value = (1.5 * raw.astype(F32) - 0.5 * nn(gram, raw)) / jnp.sqrt(gscale)
    raw = value.astype(BF)
    gram = nt(raw, raw).astype(BF)
    newer[...] = 1.5 * value - 0.5 * nn(gram, raw)
    lower[...] = newer[...].astype(BF)
    start = pl.multiple_of((4 * ax + 2 * low) * count, count)
    size = 2 * count
    if not last:
        start = pl.multiple_of(start + ay * count, count)
        size = count
    raw = lower[...]
    gram = nt(lower[pl.ds(start, size), :], raw).astype(BF)
    weights = 1.5 * newer[pl.ds(start, size), :] - 0.5 * nn(gram, raw)
    for copy in copies:
        copy.wait()
    if last:
        outs[0][...] = weights
        width = white.shape[2]
        for k in range(chunks):
            place = 2 * (ax ^ (k >> 1)) + (low ^ (k & 1))
            outs[1][:, pl.ds(pl.multiple_of(place * width, width), width)] = nn(
                weights.astype(BF), white[k]
            ).astype(BF)
    else:
        total, slope = step(weights, white[0])
        for k in range(1, chunks):
            pulled, part = step(weights, white[k])
            total += pulled
            slope += part
        outs[0][...] = total - slope * weights


def shards(data, projection, initial):
    comps = lax.axis_size("comp")
    voxels = data.shape[1] * lax.axis_size("vox")
    vox, comp = lax.axis_index("vox"), lax.axis_index("comp")
    index = vox * comps + comp
    all_bits = (lax.axis_size("vox") * comps).bit_length() - 1
    low, across, near = 1, 2, comps
    far = [1 << k for k in range(near.bit_length(), all_bits)]
    at = jnp.stack([comp & 1, comp >> 1, vox & 1]).astype(jnp.int32)
    rows = projection.shape[0]
    size = data.shape[1] // comps

    def columns(x):
        start = (x * 2 + (1 - at[0])) * size
        return flip(lax.dynamic_slice_in_dim(data, start, size, 1), low)

    other = flip(projection, low)
    sent = run(
        functools.partial(project_kernel, True),
        shape((rows, size), BF),
        (at, projection, data, other, columns(1 - at[1])),
    )
    kept = run(
        functools.partial(project_kernel, False),
        shape((rows, size), F32),
        (at, projection, data, other, columns(at[1])),
    )
    reduced = (kept + flip(sent, across).astype(F32)).astype(BF)

    block = rows // 4
    piece = 5 * block // 4
    small = shape((piece, block), BF)
    there = flip(reduced, low)
    own, by, bx, bxy = run(
        covar_kernel,
        (shape((piece, block), F32), small, small, small),
        (at, reduced, there),
        scratch=[pltpu.VMEM((rows, 2 * size), BF), pltpu.VMEM((5 * block, block), F32)],
    )
    own = own + flip(by, near).astype(F32)
    own = own + flip(bx, across).astype(F32)
    own = own + flip(bxy, across | near).astype(F32)

    reduced, own = lax.optimization_barrier((reduced, own))
    at_x, at_y = flip(reduced, across), flip(reduced, near)
    packed = sum_over(own, far).astype(BF)
    packed = spread(packed, across, near)
    packed, reduced, at_x, at_y = lax.optimization_barrier((packed, reduced, at_x, at_y))
    at_xy = flip(reduced, across | near)
    whiten = run(
        functools.partial(whiten_kernel, voxels),
        shape((rows, rows), BF),
        (at, packed, flip(packed, low)),
        scratch=[pltpu.VMEM((2, 5 * block, block), F32), pltpu.VMEM((rows, rows), F32)],
    )

    count = initial.shape[0] // 2
    weights = lax.dynamic_slice_in_dim(initial, at[2] * count, count, 0)
    outs = (
        shape((4, rows, size), BF),
        shape((count, rows), F32),
        shape((count, 1), F32),
    )
    blocks = (reduced, there, at_x, flip(at_x, low))
    white_here, total, slope = run(
        functools.partial(apply_kernel, False),
        outs,
        (whiten, *blocks, weights),
        specs=[VMEM] * 6,
    )
    blocks = (at_y, flip(at_y, low), at_xy, flip(at_xy, low))
    white_there, newer, _ = run(
        functools.partial(apply_kernel, True),
        outs,
        (whiten, *blocks, total, slope, weights),
        specs=[VMEM] * 8,
    )
    whites = (white_here, white_there)

    for turn in range(ICA_ITERS):
        last = turn == ICA_ITERS - 1
        stacked = spread(sum_over(newer, far).astype(BF), across, near)
        used = whites[:1] if last else whites
        outs = (
            (shape((2 * count, rows), F32), shape((2 * count, data.shape[1]), BF))
            if last
            else shape((count, rows), F32)
        )
        newer = run(
            functools.partial(decor_kernel, last),
            outs,
            (at, stacked, flip(stacked, low), *used),
            specs=[SMEM, VMEM, VMEM] + [ANY] * len(used),
            scratch=[
                pltpu.VMEM((rows, rows), F32),
                pltpu.VMEM((rows, rows), BF),
                pltpu.VMEM((4 * len(used), rows, size), BF),
                pltpu.SemaphoreType.DMA((2,)),
            ],
        )
    return newer


def solution(mesh):
    return jax.shard_map(
        shards,
        mesh=mesh,
        in_specs=(P("comp", "vox"), P(None, "comp"), P("comp", None)),
        out_specs=(P("comp", None), P("comp", "vox")),
        check_vma=False,
    )
```

```python
import functools

import jax
import jax.numpy as jnp
from jax import lax
from jax.experimental import pallas as pl
from jax.experimental.pallas import tpu as pltpu
from jax.sharding import PartitionSpec as P

ICA_ITERS = 2
AXES = ("vox", "comp")
BF = jnp.bfloat16
F32 = jnp.float32
MIB = 1 << 20


def nn(left, right):
    return jnp.dot(left, right, preferred_element_type=F32)


def nt(left, right):
    return lax.dot_general(
        left, right, (((1,), (1,)), ((), ())), preferred_element_type=F32
    )


def rounded(x):
    return lax.reduce_precision(x, 8, 7)


def flip(x, mask):
    count = lax.axis_size("vox") * lax.axis_size("comp")
    return lax.ppermute(x, AXES, [(i, i ^ mask) for i in range(count)])


def sum_over(x, masks):
    for k in range(0, len(masks), 2):
        sent = x.astype(BF)
        x = rounded(x) + flip(sent, masks[k]).astype(F32)
        if k + 1 < len(masks):
            x = x + (
                flip(sent, masks[k + 1]).astype(F32)
                + flip(sent, masks[k] | masks[k + 1]).astype(F32)
            )
    return x


def spread(x, across, near):
    return jnp.stack([x, flip(x, near), flip(x, across), flip(x, across | near)])


VMEM = pl.BlockSpec(memory_space=pltpu.VMEM)
SMEM = pl.BlockSpec(memory_space=pltpu.SMEM)
ANY = pl.BlockSpec(memory_space=pl.ANY)


def run(kernel, outs, args, specs=None, scratch=(), limit=24):
    return pl.pallas_call(
        kernel,
        out_shape=outs,
        in_specs=specs or [SMEM] + [VMEM] * (len(args) - 1),
        out_specs=jax.tree.map(lambda _: VMEM, outs),
        scratch_shapes=list(scratch),
        compiler_params=pltpu.CompilerParams(vmem_limit_bytes=limit * MIB),
    )(*args)


def shape(dims, dtype):
    return jax.ShapeDtypeStruct(dims, dtype)


def own_kernel(at, left_ref, right_ref, out_ref):
    size = out_ref.shape[2]
    for k, across in enumerate((1 - at[1], at[1])):
        start = pl.multiple_of((across * 2 + at[0]) * size, size)
        out_ref[k] = nn(left_ref[...], right_ref[:, pl.ds(start, size)])


def project_kernel(k, left_ref, right_ref, part_ref, out_ref):
    out_ref[...] = (part_ref[k] + nn(left_ref[...], right_ref[...])).astype(out_ref.dtype)


def covar_kernel(at, here_ref, there_ref, own_ref, y_ref, x_ref, xy_ref, both, pack):
    rows, size = here_ref.shape
    block = rows // 4
    both[:, :size] = here_ref[...]
    both[:, size:] = there_ref[...]

    def part(k):
        return both[pl.ds(pl.multiple_of(k * block, block), block), :]

    low = at[0]
    first, second = part(2 * low), part(2 * low + 1)
    third = part(2 - 2 * low)
    pack[0 * block : 1 * block] = nt(first, first)
    pack[1 * block : 2 * block] = nt(first, second)
    pack[2 * block : 3 * block] = nt(second, second)
    pack[3 * block : 4 * block] = nt(second, third)
    pack[4 * block : 5 * block] = nt(part(low), part(2 + low))
    piece = own_ref.shape[0]

    def quarter(i, j):
        return pack[pl.ds(pl.multiple_of((2 * i + j) * piece, piece), piece), :]

    ax, ay = at[1], at[2]
    own_ref[...] = quarter(ax, ay)
    y_ref[...] = quarter(ax, 1 - ay).astype(BF)
    x_ref[...] = quarter(1 - ax, ay).astype(BF)
    xy_ref[...] = quarter(1 - ax, 1 - ay).astype(BF)


def whiten_kernel(voxels, at, mine_ref, other_ref, out_ref, packs, covar):
    piece = mine_ref.shape[1]
    block = mine_ref.shape[2]
    rows = covar.shape[0]
    low, ax, ay = at[0], at[1], at[2]
    for k in range(4):
        i, j = ax ^ (k >> 1), ay ^ (k & 1)
        place = pl.ds(pl.multiple_of((2 * i + j) * piece, piece), piece)
        packs[low, place, :] = mine_ref[k].astype(F32) * (1.0 / voxels)
        packs[1 - low, place, :] = other_ref[k].astype(F32) * (1.0 / voxels)

    squares = jnp.zeros((block, block), F32)

    def put(i, j, core, k):
        value = packs[core, k * block : (k + 1) * block, :]
        covar[i * block : (i + 1) * block, j * block : (j + 1) * block] = value
        if i == j:
            return value * value
        covar[j * block : (j + 1) * block, i * block : (i + 1) * block] = value.T
        return 2.0 * (value * value)

    for core in (0, 1):
        a, b, c = 2 * core, 2 * core + 1, 2 - 2 * core
        squares += put(a, a, core, 0)
        squares += put(a, b, core, 1)
        squares += put(b, b, core, 2)
        squares += put(b, c, core, 3)
        squares += put(core, 2 + core, core, 4)

    cscale = jnp.sqrt(jnp.sum(squares, keepdims=True) + 1e-06)
    y = covar[...] * (1.0 / cscale)
    eye = (
        lax.broadcasted_iota(jnp.int32, (rows, rows), 0)
        == lax.broadcasted_iota(jnp.int32, (rows, rows), 1)
    ).astype(F32)
    yb = y.astype(BF)
    square = nn(yb, yb)
    squared = square.astype(BF)
    rest = -2.4375 * y + 1.6875 * square
    rest += nn(squared, (0.0625 * square - 0.5625 * y).astype(BF))
    restb = rest.astype(BF)
    left = 2.25 * y + nn(yb, restb)
    right = 4.5 * rest + nn(restb, restb)
    z3 = 3.375 * eye + 1.5 * rest - 0.5 * (
        5.0625 * left + nn(left.astype(BF), right.astype(BF))
    )
    out_ref[...] = (z3 * lax.rsqrt(cscale)).astype(BF)


def step(weights, blocks):
    low = weights.astype(BF)
    bents = [jnp.tanh(nn(low, block)) for block in blocks]
    pulled = nt(bents[0].astype(BF), blocks[0])
    slopes = 1.0 - bents[0] * bents[0]
    for bent, block in zip(bents[1:], blocks[1:]):
        pulled += nt(bent.astype(BF), block)
        slopes += 1.0 - bent * bent
    return pulled, jnp.sum(slopes, axis=1, keepdims=True)


def apply_kernel(part, whiten_ref, *refs):
    blocks, (weights_ref, white_ref, total_ref, slope_ref) = refs[:4], refs[-4:]
    weights = weights_ref[...]
    whites = [nn(whiten_ref[...], block[...]).astype(BF) for block in blocks]
    for k, white in enumerate(whites):
        white_ref[k] = white
    total, slope = step(weights, whites)
    if part:
        slope += refs[5][...]
        total += refs[4][...] - slope * weights
    total_ref[...] = total
    slope_ref[...] = slope


def decor_kernel(last, at, mine_ref, other_ref, *refs):
    sources = 1 if last else 2
    whites, outs, (newer, lower, white, sem) = refs[:sources], refs[sources:-4], refs[-4:]
    count = mine_ref.shape[1]
    low, ax, ay = at[0], at[1], at[2]
    chunks = white.shape[0]
    copies = [
        pltpu.make_async_copy(ref, white.at[pl.ds(4 * k, 4)], sem.at[k])
        for k, ref in enumerate(whites)
    ]
    for copy in copies:
        copy.start()
    for k in range(4):
        i, j = ax ^ (k >> 1), ay ^ (k & 1)
        for ref, core in ((mine_ref, low), (other_ref, 1 - low)):
            start = pl.multiple_of((4 * i + 2 * core + j) * count, count)
            lower[pl.ds(start, count), :] = ref[k]

    raw = lower[...]
    gram = nt(raw, raw)
    gscale = jnp.sqrt(jnp.sum(gram * gram, keepdims=True) + 1e-06)
    value = 1.5 * raw.astype(F32) - (0.5 / gscale) * nn(gram.astype(BF), raw)
    value = value * lax.rsqrt(gscale)
    raw = value.astype(BF)
    gram = nt(raw, raw).astype(BF)
    newer[...] = 1.5 * value - 0.5 * nn(gram, raw)
    lower[...] = newer[...].astype(BF)
    start = pl.multiple_of((4 * ax + 2 * low) * count, count)
    size = 2 * count
    if not last:
        start = pl.multiple_of(start + ay * count, count)
        size = count
    raw = lower[...]
    gram = nt(lower[pl.ds(start, size), :], raw).astype(BF)
    weights = 1.5 * newer[pl.ds(start, size), :] - 0.5 * nn(gram, raw)
    for copy in copies:
        copy.wait()
    if last:
        outs[0][...] = weights
        width = white.shape[2]
        for k in range(chunks):
            place = 2 * (ax ^ (k >> 1)) + (low ^ (k & 1))
            outs[1][:, pl.ds(pl.multiple_of(place * width, width), width)] = nn(
                weights.astype(BF), white[k]
            ).astype(BF)
    else:
        total, slope = step(weights, [white[k] for k in range(chunks)])
        outs[0][...] = total - slope * weights


def shards(data, projection, initial):
    comps = lax.axis_size("comp")
    voxels = data.shape[1] * lax.axis_size("vox")
    vox, comp = lax.axis_index("vox"), lax.axis_index("comp")
    index = vox * comps + comp
    all_bits = (lax.axis_size("vox") * comps).bit_length() - 1
    low, across, near = 1, 2, comps
    far = [1 << k for k in range(near.bit_length(), all_bits)]
    at = jnp.stack([comp & 1, comp >> 1, vox & 1]).astype(jnp.int32)
    rows = projection.shape[0]
    size = data.shape[1] // comps

    def columns(data, x):
        start = (x * 2 + (1 - at[0])) * size
        return lax.dynamic_slice_in_dim(data, start, size, 1)

    other = flip(projection, low)
    away, rest = lax.optimization_barrier((columns(data, 1 - at[1]), data))
    away, stay = flip(away, low), flip(columns(rest, at[1]), low)
    part = run(own_kernel, shape((2, rows, size), F32), (at, projection, data))
    sent = run(
        functools.partial(project_kernel, 0),
        shape((rows, size), BF),
        (other, away, part),
        specs=[VMEM] * 3,
    )
    kept = run(
        functools.partial(project_kernel, 1),
        shape((rows, size), F32),
        (other, stay, part),
        specs=[VMEM] * 3,
    )
    reduced = (kept + flip(sent, across).astype(F32)).astype(BF)

    block = rows // 4
    piece = 5 * block // 4
    small = shape((piece, block), BF)
    there = flip(reduced, low)
    own, by, bx, bxy = run(
        covar_kernel,
        (shape((piece, block), F32), small, small, small),
        (at, reduced, there),
        scratch=[pltpu.VMEM((rows, 2 * size), BF), pltpu.VMEM((5 * block, block), F32)],
    )
    own = own + flip(by, near).astype(F32)
    own = own + flip(bx, across).astype(F32)
    own = own + flip(bxy, across | near).astype(F32)

    reduced, own = lax.optimization_barrier((reduced, own))
    at_x, at_y = flip(reduced, across), flip(reduced, near)
    packed = sum_over(own, far).astype(BF)
    packed, reduced = lax.optimization_barrier((packed, reduced))
    at_xy = flip(reduced, across | near)
    packed = spread(packed, across, near)
    mate = flip(packed, low)
    mate, at_x, at_y = lax.optimization_barrier((mate, at_x, at_y))
    at_xc, at_yc = flip(at_x, low), flip(at_y, low)
    whiten = run(
        functools.partial(whiten_kernel, voxels),
        shape((rows, rows), BF),
        (at, packed, mate),
        scratch=[pltpu.VMEM((2, 5 * block, block), F32), pltpu.VMEM((rows, rows), F32)],
    )
    whiten, at_xy = lax.optimization_barrier((whiten, at_xy))

    count = initial.shape[0] // 2
    weights = lax.dynamic_slice_in_dim(initial, at[2] * count, count, 0)
    outs = (
        shape((4, rows, size), BF),
        shape((count, rows), F32),
        shape((count, 1), F32),
    )
    blocks = (reduced, there, at_x, at_xc)
    white_here, total, slope = run(
        functools.partial(apply_kernel, False),
        outs,
        (whiten, *blocks, weights),
        specs=[VMEM] * 6,
    )
    blocks = (at_y, at_yc, at_xy, flip(at_xy, low))
    white_there, newer, _ = run(
        functools.partial(apply_kernel, True),
        outs,
        (whiten, *blocks, total, slope, weights),
        specs=[VMEM] * 8,
    )
    whites = (white_here, white_there)

    for turn in range(ICA_ITERS):
        last = turn == ICA_ITERS - 1
        stacked = spread(sum_over(newer, far).astype(BF), across, near)
        used = whites[:1] if last else whites
        outs = (
            (shape((2 * count, rows), F32), shape((2 * count, data.shape[1]), BF))
            if last
            else shape((count, rows), F32)
        )
        newer = run(
            functools.partial(decor_kernel, last),
            outs,
            (at, stacked, flip(stacked, low), *used),
            specs=[SMEM, VMEM, VMEM] + [ANY] * len(used),
            scratch=[
                pltpu.VMEM((rows, rows), F32),
                pltpu.VMEM((rows, rows), BF),
                pltpu.VMEM((4 * len(used), rows, size), BF),
                pltpu.SemaphoreType.DMA((2,)),
            ],
        )
    return newer


def solution(mesh):
    return jax.shard_map(
        shards,
        mesh=mesh,
        in_specs=(P("comp", "vox"), P(None, "comp"), P("comp", None)),
        out_specs=(P("comp", None), P("comp", "vox")),
        check_vma=False,
    )
```

```python
import functools

import jax
import jax.numpy as jnp
from jax import lax
from jax.experimental import pallas as pl
from jax.experimental.pallas import tpu as pltpu
from jax.sharding import PartitionSpec as P

ICA_ITERS = 2
AXES = ("vox", "comp")
BF = jnp.bfloat16
F32 = jnp.float32
MIB = 1 << 20


def nn(left, right):
    return jnp.dot(left, right, preferred_element_type=F32)


def nt(left, right):
    return lax.dot_general(
        left, right, (((1,), (1,)), ((), ())), preferred_element_type=F32
    )


def rounded(x):
    return lax.reduce_precision(x, 8, 7)


def flip(x, mask):
    count = lax.axis_size("vox") * lax.axis_size("comp")
    return lax.ppermute(x, AXES, [(i, i ^ mask) for i in range(count)])


def sum_over(x, masks):
    for k in range(0, len(masks), 2):
        sent = x.astype(BF)
        x = rounded(x) + flip(sent, masks[k]).astype(F32)
        if k + 1 < len(masks):
            x = x + (
                flip(sent, masks[k + 1]).astype(F32)
                + flip(sent, masks[k] | masks[k + 1]).astype(F32)
            )
    return x


def spread(x, across, near):
    return jnp.stack([x, flip(x, near), flip(x, across), flip(x, across | near)])


VMEM = pl.BlockSpec(memory_space=pltpu.VMEM)
SMEM = pl.BlockSpec(memory_space=pltpu.SMEM)
ANY = pl.BlockSpec(memory_space=pl.ANY)


def run(kernel, outs, args, specs=None, scratch=(), limit=24):
    return pl.pallas_call(
        kernel,
        out_shape=outs,
        in_specs=specs or [SMEM] + [VMEM] * (len(args) - 1),
        out_specs=jax.tree.map(lambda _: VMEM, outs),
        scratch_shapes=list(scratch),
        compiler_params=pltpu.CompilerParams(vmem_limit_bytes=limit * MIB),
    )(*args)


def shape(dims, dtype):
    return jax.ShapeDtypeStruct(dims, dtype)


def own_kernel(at, left_ref, right_ref, out_ref):
    size = out_ref.shape[2]
    for k, across in enumerate((1 - at[1], at[1])):
        start = pl.multiple_of((across * 2 + at[0]) * size, size)
        out_ref[k] = nn(left_ref[...], right_ref[:, pl.ds(start, size)])


def project_kernel(k, left_ref, right_ref, part_ref, out_ref):
    out_ref[...] = (part_ref[k] + nn(left_ref[...], right_ref[...])).astype(out_ref.dtype)


def covar_kernel(at, here_ref, there_ref, own_ref, y_ref, x_ref, xy_ref, both, pack):
    rows, size = here_ref.shape
    block = rows // 4
    both[:, :size] = here_ref[...]
    both[:, size:] = there_ref[...]

    def part(k):
        return both[pl.ds(pl.multiple_of(k * block, block), block), :]

    low = at[0]
    first, second = part(2 * low), part(2 * low + 1)
    third = part(2 - 2 * low)
    pack[0 * block : 1 * block] = nt(first, first)
    pack[1 * block : 2 * block] = nt(first, second)
    pack[2 * block : 3 * block] = nt(second, second)
    pack[3 * block : 4 * block] = nt(second, third)
    pack[4 * block : 5 * block] = nt(part(low), part(2 + low))
    piece = own_ref.shape[0]

    def quarter(i, j):
        return pack[pl.ds(pl.multiple_of((2 * i + j) * piece, piece), piece), :]

    ax, ay = at[1], at[2]
    own_ref[...] = quarter(ax, ay)
    y_ref[...] = quarter(ax, 1 - ay).astype(BF)
    x_ref[...] = quarter(1 - ax, ay).astype(BF)
    xy_ref[...] = quarter(1 - ax, 1 - ay).astype(BF)


def whiten_kernel(voxels, at, mine_ref, other_ref, out_ref, packs, covar):
    piece = mine_ref.shape[1]
    block = mine_ref.shape[2]
    rows = covar.shape[0]
    low, ax, ay = at[0], at[1], at[2]
    for k in range(4):
        i, j = ax ^ (k >> 1), ay ^ (k & 1)
        place = pl.ds(pl.multiple_of((2 * i + j) * piece, piece), piece)
        packs[low, place, :] = mine_ref[k].astype(F32) * (1.0 / voxels)
        packs[1 - low, place, :] = other_ref[k].astype(F32) * (1.0 / voxels)

    squares = jnp.zeros((block, block), F32)

    def put(i, j, core, k):
        value = packs[core, k * block : (k + 1) * block, :]
        covar[i * block : (i + 1) * block, j * block : (j + 1) * block] = value
        if i == j:
            return value * value
        covar[j * block : (j + 1) * block, i * block : (i + 1) * block] = value.T
        return 2.0 * (value * value)

    for core in (0, 1):
        a, b, c = 2 * core, 2 * core + 1, 2 - 2 * core
        squares += put(a, a, core, 0)
        squares += put(a, b, core, 1)
        squares += put(b, b, core, 2)
        squares += put(b, c, core, 3)
        squares += put(core, 2 + core, core, 4)

    cscale = jnp.sqrt(jnp.sum(squares, keepdims=True) + 1e-06)
    y = covar[...] * (1.0 / cscale)
    eye = (
        lax.broadcasted_iota(jnp.int32, (rows, rows), 0)
        == lax.broadcasted_iota(jnp.int32, (rows, rows), 1)
    ).astype(F32)
    yb = y.astype(BF)
    square = nn(yb, yb)
    squared = square.astype(BF)
    rest = -2.4375 * y + 1.6875 * square
    rest += nn(squared, (0.0625 * square - 0.5625 * y).astype(BF))
    restb = rest.astype(BF)
    left = 2.25 * y + nn(yb, restb)
    right = 4.5 * rest + nn(restb, restb)
    z3 = 3.375 * eye + 1.5 * rest - 0.5 * (
        5.0625 * left + nn(left.astype(BF), right.astype(BF))
    )
    out_ref[...] = (z3 * lax.rsqrt(cscale)).astype(BF)


def step(weights, blocks):
    low = weights.astype(BF)
    bents = [jnp.tanh(nn(low, block)) for block in blocks]
    pulled = nt(bents[0].astype(BF), blocks[0])
    slopes = 1.0 - bents[0] * bents[0]
    for bent, block in zip(bents[1:], blocks[1:]):
        pulled += nt(bent.astype(BF), block)
        slopes += 1.0 - bent * bent
    return pulled, jnp.sum(slopes, axis=1, keepdims=True)


def apply_kernel(part, whiten_ref, *refs):
    blocks, (weights_ref, white_ref, total_ref, slope_ref) = refs[:4], refs[-4:]
    weights = weights_ref[...]
    whites = [nn(whiten_ref[...], block[...]).astype(BF) for block in blocks]
    for k, white in enumerate(whites):
        white_ref[k] = white
    total, slope = step(weights, whites)
    if part:
        slope += refs[5][...]
        total += refs[4][...] - slope * weights
    total_ref[...] = total
    slope_ref[...] = slope


def decor_kernel(last, at, mine_ref, other_ref, *refs):
    whites, outs, (newer, lower, white, sem) = refs[:2], refs[2:-4], refs[-4:]
    count = mine_ref.shape[1]
    low, ax, ay = at[0], at[1], at[2]
    chunks = white.shape[0]
    first = 3 if last else 4
    copies = [
        pltpu.make_async_copy(
            ref.at[pl.ds(0, size)], white.at[pl.ds(start, size)], sem.at[k]
        )
        for k, (ref, start, size) in enumerate(
            zip(whites, (0, first), (first, chunks - first))
        )
    ]
    for copy in copies:
        copy.start()
    for k in range(4):
        i, j = ax ^ (k >> 1), ay ^ (k & 1)
        for ref, core in ((mine_ref, low), (other_ref, 1 - low)):
            start = pl.multiple_of((4 * i + 2 * core + j) * count, count)
            lower[pl.ds(start, count), :] = ref[k]

    raw = lower[...]
    gram = nt(raw, raw)
    gscale = jnp.sqrt(jnp.sum(gram * gram, keepdims=True) + 1e-06)
    value = 1.5 * raw.astype(F32) - (0.5 / gscale) * nn(gram.astype(BF), raw)
    value = value * lax.rsqrt(gscale)
    raw = value.astype(BF)
    gram = nt(raw, raw).astype(BF)
    newer[...] = 1.5 * value - 0.5 * nn(gram, raw)
    lower[...] = newer[...].astype(BF)
    start = pl.multiple_of((4 * ax + 2 * low) * count, count)
    size = 2 * count
    if not last:
        start = pl.multiple_of(start + ay * count, count)
        size = count
    raw = lower[...]
    gram = nt(lower[pl.ds(start, size), :], raw).astype(BF)
    weights = 1.5 * newer[pl.ds(start, size), :] - 0.5 * nn(gram, raw)
    for copy in copies:
        copy.wait()
    if last:
        outs[0][...] = weights
        width = white.shape[2]
        for k in range(chunks):
            place = 2 * (ax ^ (k >> 1)) + (low ^ (k & 1))
            outs[1][:, pl.ds(pl.multiple_of(place * width, width), width)] = nn(
                weights.astype(BF), white[k]
            ).astype(BF)
    else:
        total, slope = step(weights, [white[k] for k in range(chunks)])
        outs[0][...] = total - slope * weights


def shards(data, projection, initial):
    comps = lax.axis_size("comp")
    voxels = data.shape[1] * lax.axis_size("vox")
    vox, comp = lax.axis_index("vox"), lax.axis_index("comp")
    index = vox * comps + comp
    all_bits = (lax.axis_size("vox") * comps).bit_length() - 1
    low, across, near = 1, 2, comps
    far = [1 << k for k in range(near.bit_length(), all_bits)]
    at = jnp.stack([comp & 1, comp >> 1, vox & 1]).astype(jnp.int32)
    rows = projection.shape[0]
    size = data.shape[1] // comps

    def columns(x):
        start = (x * 2 + (1 - at[0])) * size
        return flip(lax.dynamic_slice_in_dim(data, start, size, 1), low)

    other = flip(projection, low)
    away, stay = columns(1 - at[1]), columns(at[1])
    part = run(own_kernel, shape((2, rows, size), F32), (at, projection, data))
    sent = run(
        functools.partial(project_kernel, 0),
        shape((rows, size), BF),
        (other, away, part),
        specs=[VMEM] * 3,
    )
    kept = run(
        functools.partial(project_kernel, 1),
        shape((rows, size), F32),
        (other, stay, part),
        specs=[VMEM] * 3,
    )
    reduced = (kept + flip(sent, across).astype(F32)).astype(BF)

    block = rows // 4
    piece = 5 * block // 4
    small = shape((piece, block), BF)
    there = flip(reduced, low)
    own, by, bx, bxy = run(
        covar_kernel,
        (shape((piece, block), F32), small, small, small),
        (at, reduced, there),
        scratch=[pltpu.VMEM((rows, 2 * size), BF), pltpu.VMEM((5 * block, block), F32)],
    )
    own = own + flip(by, near).astype(F32)
    own = own + flip(bx, across).astype(F32)
    own = own + flip(bxy, across | near).astype(F32)

    reduced, own = lax.optimization_barrier((reduced, own))
    at_x, at_y = flip(reduced, across), flip(reduced, near)
    packed = sum_over(own, far).astype(BF)
    packed, reduced = lax.optimization_barrier((packed, reduced))
    at_xy = flip(reduced, across | near)
    packed = spread(packed, across, near)
    packed, at_x, at_y = lax.optimization_barrier((packed, at_x, at_y))
    mate = flip(packed, low)
    whiten = run(
        functools.partial(whiten_kernel, voxels),
        shape((rows, rows), BF),
        (at, packed, mate),
        scratch=[pltpu.VMEM((2, 5 * block, block), F32), pltpu.VMEM((rows, rows), F32)],
    )
    whiten, at_xy = lax.optimization_barrier((whiten, at_xy))

    count = initial.shape[0] // 2
    weights = lax.dynamic_slice_in_dim(initial, at[2] * count, count, 0)
    outs = (
        shape((4, rows, size), BF),
        shape((count, rows), F32),
        shape((count, 1), F32),
    )
    blocks = (reduced, there, at_x, at_y)
    white_here, total, slope = run(
        functools.partial(apply_kernel, False),
        outs,
        (whiten, *blocks, weights),
        specs=[VMEM] * 6,
    )
    blocks = (flip(at_x, low), flip(at_y, low), at_xy, flip(at_xy, low))
    white_there, newer, _ = run(
        functools.partial(apply_kernel, True),
        outs,
        (whiten, *blocks, total, slope, weights),
        specs=[VMEM] * 8,
    )
    whites = (white_here, white_there)

    for turn in range(ICA_ITERS):
        last = turn == ICA_ITERS - 1
        stacked = spread(sum_over(newer, far).astype(BF), across, near)
        chunks = 4 if last else 8
        outs = (
            (shape((2 * count, rows), F32), shape((2 * count, data.shape[1]), BF))
            if last
            else shape((count, rows), F32)
        )
        newer = run(
            functools.partial(decor_kernel, last),
            outs,
            (at, stacked, flip(stacked, low), *whites),
            specs=[SMEM, VMEM, VMEM] + [ANY] * 2,
            scratch=[
                pltpu.VMEM((rows, rows), F32),
                pltpu.VMEM((rows, rows), BF),
                pltpu.VMEM((chunks, rows, size), BF),
                pltpu.SemaphoreType.DMA((2,)),
            ],
        )
    return newer


def solution(mesh):
    return jax.shard_map(
        shards,
        mesh=mesh,
        in_specs=(P("comp", "vox"), P(None, "comp"), P("comp", None)),
        out_specs=(P("comp", None), P("comp", "vox")),
        check_vma=False,
    )
```

```python
import functools

import jax
import jax.numpy as jnp
from jax import lax
from jax.experimental import pallas as pl
from jax.experimental.pallas import tpu as pltpu
from jax.sharding import PartitionSpec as P

ICA_ITERS = 2
AXES = ("vox", "comp")
BF = jnp.bfloat16
F32 = jnp.float32
MIB = 1 << 20


def nn(left, right):
    return jnp.dot(left, right, preferred_element_type=F32)


def nt(left, right):
    return lax.dot_general(
        left, right, (((1,), (1,)), ((), ())), preferred_element_type=F32
    )


def rounded(x):
    return lax.reduce_precision(x, 8, 7)


def flip(x, mask):
    count = lax.axis_size("vox") * lax.axis_size("comp")
    return lax.ppermute(x, AXES, [(i, i ^ mask) for i in range(count)])


def sum_over(x, masks):
    for k in range(0, len(masks), 2):
        sent = x.astype(BF)
        x = rounded(x) + flip(sent, masks[k]).astype(F32)
        if k + 1 < len(masks):
            x = x + (
                flip(sent, masks[k + 1]).astype(F32)
                + flip(sent, masks[k] | masks[k + 1]).astype(F32)
            )
    return x


def spread(x, across, near):
    return jnp.stack([x, flip(x, near), flip(x, across), flip(x, across | near)])


VMEM = pl.BlockSpec(memory_space=pltpu.VMEM)
SMEM = pl.BlockSpec(memory_space=pltpu.SMEM)
HBM = pl.BlockSpec(memory_space=pltpu.HBM)


def run(kernel, outs, args, specs=None, scratch=(), limit=24):
    return pl.pallas_call(
        kernel,
        out_shape=outs,
        in_specs=specs or [SMEM] + [VMEM] * (len(args) - 1),
        out_specs=jax.tree.map(lambda _: VMEM, outs),
        scratch_shapes=list(scratch),
        compiler_params=pltpu.CompilerParams(vmem_limit_bytes=limit * MIB),
    )(*args)


def shape(dims, dtype):
    return jax.ShapeDtypeStruct(dims, dtype)


def project_kernel(left_ref, right_ref, mate_left_ref, mate_right_ref, out_ref):
    total = nn(left_ref[...], right_ref[...])
    total += nn(mate_left_ref[...], mate_right_ref[...])
    out_ref[...] = total.astype(out_ref.dtype)


def covar_kernel(at, here_ref, there_ref, own_ref, y_ref, x_ref, xy_ref, pack):
    rows = here_ref.shape[0]
    block = rows // 4

    def put(k, i, j):
        total = 0.0
        for ref in (here_ref, there_ref):
            left = ref[pl.ds(pl.multiple_of(i * block, block), block), :]
            right = ref[pl.ds(pl.multiple_of(j * block, block), block), :]
            total += nt(left, right)
        pack[k * block : (k + 1) * block] = total

    low = at[0]
    first, second, third = 2 * low, 2 * low + 1, 2 - 2 * low
    put(0, first, first)
    put(1, first, second)
    put(2, second, second)
    put(3, second, third)
    put(4, low, 2 + low)
    piece = own_ref.shape[0]

    def quarter(i, j):
        return pack[pl.ds(pl.multiple_of((2 * i + j) * piece, piece), piece), :]

    ax, ay = at[1], at[2]
    own_ref[...] = quarter(ax, ay)
    y_ref[...] = quarter(ax, 1 - ay).astype(BF)
    x_ref[...] = quarter(1 - ax, ay).astype(BF)
    xy_ref[...] = quarter(1 - ax, 1 - ay).astype(BF)


def whiten_kernel(voxels, at, mine_ref, other_ref, out_ref, packs, covar):
    piece = mine_ref.shape[1]
    block = mine_ref.shape[2]
    rows = covar.shape[0]
    low, ax, ay = at[0], at[1], at[2]
    for k in range(4):
        i, j = ax ^ (k >> 1), ay ^ (k & 1)
        place = pl.ds(pl.multiple_of((2 * i + j) * piece, piece), piece)
        packs[low, place, :] = mine_ref[k].astype(F32) * (1.0 / voxels)
        packs[1 - low, place, :] = other_ref[k].astype(F32) * (1.0 / voxels)

    squares = jnp.zeros((block, block), F32)

    def put(i, j, core, k):
        value = packs[core, k * block : (k + 1) * block, :]
        covar[i * block : (i + 1) * block, j * block : (j + 1) * block] = value
        if i == j:
            return value * value
        covar[j * block : (j + 1) * block, i * block : (i + 1) * block] = value.T
        return 2.0 * (value * value)

    for core in (0, 1):
        a, b, c = 2 * core, 2 * core + 1, 2 - 2 * core
        squares += put(a, a, core, 0)
        squares += put(a, b, core, 1)
        squares += put(b, b, core, 2)
        squares += put(b, c, core, 3)
        squares += put(core, 2 + core, core, 4)

    cscale = jnp.sqrt(jnp.sum(squares, keepdims=True) + 1e-06)
    y = covar[...] * (1.0 / cscale)
    eye = (
        lax.broadcasted_iota(jnp.int32, (rows, rows), 0)
        == lax.broadcasted_iota(jnp.int32, (rows, rows), 1)
    ).astype(F32)
    yb = y.astype(BF)
    square = nn(yb, yb)
    squared = square.astype(BF)
    rest = -2.4375 * y + 1.6875 * square
    rest += nn(squared, (0.0625 * square - 0.5625 * y).astype(BF))
    restb = rest.astype(BF)
    left = 2.25 * y + nn(yb, restb)
    right = 4.5 * rest + nn(restb, restb)
    z3 = 3.375 * eye + 1.5 * rest - 0.5 * (
        5.0625 * left + nn(left.astype(BF), right.astype(BF))
    )
    out_ref[...] = (z3 * lax.rsqrt(cscale)).astype(BF)


def step(weights, blocks):
    low = weights.astype(BF)
    bents = [jnp.tanh(nn(low, block)) for block in blocks]
    pulled = nt(bents[0].astype(BF), blocks[0])
    slopes = 1.0 - bents[0] * bents[0]
    for bent, block in zip(bents[1:], blocks[1:]):
        pulled += nt(bent.astype(BF), block)
        slopes += 1.0 - bent * bent
    return pulled, jnp.sum(slopes, axis=1, keepdims=True)


def apply_kernel(part, whiten_ref, *refs):
    blocks, (weights_ref, white_ref, total_ref, slope_ref) = refs[:4], refs[-4:]
    weights = weights_ref[...]
    whites = [nn(whiten_ref[...], block[...]).astype(BF) for block in blocks]
    for k, white in enumerate(whites):
        white_ref[k] = white
    total, slope = step(weights, whites)
    if part:
        slope += refs[5][...]
        total += refs[4][...] - slope * weights
    total_ref[...] = total
    slope_ref[...] = slope


def decor_kernel(last, at, mine_ref, other_ref, *refs):
    whites, outs, (newer, lower, white, sem) = refs[:2], refs[2:-4], refs[-4:]
    count = mine_ref.shape[1]
    low, ax, ay = at[0], at[1], at[2]
    chunks = white.shape[0]
    first = 3 if last else 4
    copies = [
        pltpu.make_async_copy(
            ref.at[pl.ds(0, size)], white.at[pl.ds(start, size)], sem.at[k]
        )
        for k, (ref, start, size) in enumerate(
            zip(whites, (0, first), (first, chunks - first))
        )
    ]
    for copy in copies:
        copy.start()
    for k in range(4):
        i, j = ax ^ (k >> 1), ay ^ (k & 1)
        for ref, core in ((mine_ref, low), (other_ref, 1 - low)):
            start = pl.multiple_of((4 * i + 2 * core + j) * count, count)
            lower[pl.ds(start, count), :] = ref[k]

    raw = lower[...]
    gram = nt(raw, raw)
    gscale = jnp.sqrt(jnp.sum(gram * gram, keepdims=True) + 1e-06)
    value = 1.5 * raw.astype(F32) - (0.5 / gscale) * nn(gram.astype(BF), raw)
    value = value * lax.rsqrt(gscale)
    raw = value.astype(BF)
    gram = nt(raw, raw).astype(BF)
    newer[...] = 1.5 * value - 0.5 * nn(gram, raw)
    lower[...] = newer[...].astype(BF)
    start = pl.multiple_of((4 * ax + 2 * low) * count, count)
    size = 2 * count
    if not last:
        start = pl.multiple_of(start + ay * count, count)
        size = count
    raw = lower[...]
    gram = nt(lower[pl.ds(start, size), :], raw).astype(BF)
    weights = 1.5 * newer[pl.ds(start, size), :] - 0.5 * nn(gram, raw)
    for copy in copies:
        copy.wait()
    if last:
        outs[0][...] = weights
        width = white.shape[2]
        for k in range(chunks):
            place = 2 * (ax ^ (k >> 1)) + (low ^ (k & 1))
            outs[1][:, pl.ds(pl.multiple_of(place * width, width), width)] = nn(
                weights.astype(BF), white[k]
            ).astype(BF)
    else:
        total, slope = step(weights, [white[k] for k in range(chunks)])
        outs[0][...] = total - slope * weights


def shards(data, projection, initial):
    comps = lax.axis_size("comp")
    voxels = data.shape[1] * lax.axis_size("vox")
    vox, comp = lax.axis_index("vox"), lax.axis_index("comp")
    index = vox * comps + comp
    all_bits = (lax.axis_size("vox") * comps).bit_length() - 1
    low, across, near = 1, 2, comps
    far = [1 << k for k in range(near.bit_length(), all_bits)]
    at = jnp.stack([comp & 1, comp >> 1, vox & 1]).astype(jnp.int32)
    rows = projection.shape[0]
    size = data.shape[1] // comps

    mate = flip(projection, low)

    def columns(x, core):
        return lax.dynamic_slice_in_dim(data, (x * 2 + core) * size, size, 1)

    here, away = at[1], 1 - at[1]
    other = [columns(x, 1 - at[0]) for x in (away, here)]
    mine = [columns(x, at[0]) for x in (away, here)]
    other = [flip(block, low) for block in other]
    sent, kept = (
        run(
            project_kernel,
            shape((rows, size), kind),
            (projection, mine[k], mate, other[k]),
            specs=[VMEM] * 4,
        )
        for k, kind in enumerate((BF, F32))
    )
    reduced = (kept + flip(sent, across).astype(F32)).astype(BF)

    block = rows // 4
    piece = 5 * block // 4
    small = shape((piece, block), BF)
    there = flip(reduced, low)
    own, by, bx, bxy = run(
        covar_kernel,
        (shape((piece, block), F32), small, small, small),
        (at, reduced, there),
        scratch=[pltpu.VMEM((5 * block, block), F32)],
    )
    own = own + flip(by, near).astype(F32)
    own = own + flip(bx, across).astype(F32)
    own = own + flip(bxy, across | near).astype(F32)

    reduced, own = lax.optimization_barrier((reduced, own))
    at_x, at_y = flip(reduced, across), flip(reduced, near)
    packed = sum_over(own, far).astype(BF)
    packed, reduced = lax.optimization_barrier((packed, reduced))
    at_xy = flip(reduced, across | near)
    packed = spread(packed, across, near)
    packed, at_x, at_y = lax.optimization_barrier((packed, at_x, at_y))
    mate = flip(packed, low)
    whiten = run(
        functools.partial(whiten_kernel, voxels),
        shape((rows, rows), BF),
        (at, packed, mate),
        scratch=[pltpu.VMEM((2, 5 * block, block), F32), pltpu.VMEM((rows, rows), F32)],
    )

    whiten, at_xy = lax.optimization_barrier((whiten, at_xy))

    count = initial.shape[0] // 2
    weights = lax.dynamic_slice_in_dim(initial, at[2] * count, count, 0)
    outs = (
        shape((4, rows, size), BF),
        shape((count, rows), F32),
        shape((count, 1), F32),
    )
    blocks = (reduced, there, at_x, at_y)
    white_here, total, slope = run(
        functools.partial(apply_kernel, False),
        outs,
        (whiten, *blocks, weights),
        specs=[VMEM] * 6,
    )
    blocks = (flip(at_x, low), flip(at_y, low), at_xy, flip(at_xy, low))
    white_there, newer, _ = run(
        functools.partial(apply_kernel, True),
        outs,
        (whiten, *blocks, total, slope, weights),
        specs=[VMEM] * 8,
    )
    whites = (white_here, white_there)

    for turn in range(ICA_ITERS):
        last = turn == ICA_ITERS - 1
        stacked = spread(sum_over(newer, far).astype(BF), across, near)
        chunks = 4 if last else 8
        outs = (
            (shape((2 * count, rows), F32), shape((2 * count, data.shape[1]), BF))
            if last
            else shape((count, rows), F32)
        )
        newer = run(
            functools.partial(decor_kernel, last),
            outs,
            (at, stacked, flip(stacked, low), *whites),
            specs=[SMEM, VMEM, VMEM] + [HBM] * 2,
            scratch=[
                pltpu.VMEM((rows, rows), F32),
                pltpu.VMEM((rows, rows), BF),
                pltpu.VMEM((chunks, rows, size), BF),
                pltpu.SemaphoreType.DMA((2,)),
            ],
        )
    return newer


def solution(mesh):
    return jax.shard_map(
        shards,
        mesh=mesh,
        in_specs=(P("comp", "vox"), P(None, "comp"), P("comp", None)),
        out_specs=(P("comp", None), P("comp", "vox")),
        check_vma=False,
    )
```

```python
import functools

import jax
import jax.numpy as jnp
from jax import lax
from jax.experimental import pallas as pl
from jax.experimental.pallas import tpu as pltpu
from jax.sharding import PartitionSpec as P

ICA_ITERS = 2
AXES = ("vox", "comp")
BF = jnp.bfloat16
F32 = jnp.float32
MIB = 1 << 20


def nn(left, right):
    return jnp.dot(left, right, preferred_element_type=F32)


def nt(left, right):
    return lax.dot_general(
        left, right, (((1,), (1,)), ((), ())), preferred_element_type=F32
    )


def rounded(x):
    return lax.reduce_precision(x, 8, 7)


def flip(x, mask):
    count = lax.axis_size("vox") * lax.axis_size("comp")
    return lax.ppermute(x, AXES, [(i, i ^ mask) for i in range(count)])


def sum_over(x, masks, due=()):
    for k in range(0, len(masks), 2):
        sent = x.astype(BF)
        x = rounded(x) + flip(sent, masks[k]).astype(F32)
        if k + 1 < len(masks):
            both = flip(sent, masks[k] | masks[k + 1])
            if k == 0:
                both, *due = lax.optimization_barrier((both, *due))
            x = x + (flip(sent, masks[k + 1]).astype(F32) + both.astype(F32))
    return (x.astype(BF), *due)


def spread(x, across, near, due=()):
    both = flip(x, across | near)
    both, *due = lax.optimization_barrier((both, *due))
    return (jnp.stack([x, flip(x, near), flip(x, across), both]), *due)


VMEM = pl.BlockSpec(memory_space=pltpu.VMEM)
SMEM = pl.BlockSpec(memory_space=pltpu.SMEM)
HBM = pl.BlockSpec(memory_space=pltpu.HBM)


def run(kernel, outs, args, specs=None, scratch=(), limit=24):
    return pl.pallas_call(
        kernel,
        out_shape=outs,
        in_specs=specs or [SMEM] + [VMEM] * (len(args) - 1),
        out_specs=jax.tree.map(lambda _: VMEM, outs),
        scratch_shapes=list(scratch),
        compiler_params=pltpu.CompilerParams(vmem_limit_bytes=limit * MIB),
    )(*args)


def shape(dims, dtype):
    return jax.ShapeDtypeStruct(dims, dtype)


def project_kernel(left_ref, right_ref, mate_left_ref, mate_right_ref, out_ref):
    total = nn(left_ref[...], right_ref[...])
    total += nn(mate_left_ref[...], mate_right_ref[...])
    out_ref[...] = total.astype(out_ref.dtype)


def covar_kernel(at, here_ref, there_ref, own_ref, y_ref, x_ref, xy_ref, pack):
    rows = here_ref.shape[0]
    block = rows // 4

    def put(k, i, j):
        total = 0.0
        for ref in (here_ref, there_ref):
            left = ref[pl.ds(pl.multiple_of(i * block, block), block), :]
            right = ref[pl.ds(pl.multiple_of(j * block, block), block), :]
            total += nt(left, right)
        pack[k * block : (k + 1) * block] = total

    low = at[0]
    first, second, third = 2 * low, 2 * low + 1, 2 - 2 * low
    put(0, first, first)
    put(1, first, second)
    put(2, second, second)
    put(3, second, third)
    put(4, low, 2 + low)
    piece = own_ref.shape[0]

    def quarter(i, j):
        return pack[pl.ds(pl.multiple_of((2 * i + j) * piece, piece), piece), :]

    ax, ay = at[1], at[2]
    own_ref[...] = quarter(ax, ay)
    y_ref[...] = quarter(ax, 1 - ay).astype(BF)
    x_ref[...] = quarter(1 - ax, ay).astype(BF)
    xy_ref[...] = quarter(1 - ax, 1 - ay).astype(BF)


def whiten_kernel(voxels, at, mine_ref, other_ref, out_ref, packs, covar):
    piece = mine_ref.shape[1]
    block = mine_ref.shape[2]
    rows = covar.shape[0]
    low, ax, ay = at[0], at[1], at[2]
    for k in range(4):
        i, j = ax ^ (k >> 1), ay ^ (k & 1)
        place = pl.ds(pl.multiple_of((2 * i + j) * piece, piece), piece)
        packs[low, place, :] = mine_ref[k].astype(F32) * (1.0 / voxels)
        packs[1 - low, place, :] = other_ref[k].astype(F32) * (1.0 / voxels)

    squares = jnp.zeros((block, block), F32)

    def put(i, j, core, k):
        value = packs[core, k * block : (k + 1) * block, :]
        covar[i * block : (i + 1) * block, j * block : (j + 1) * block] = value
        if i == j:
            return value * value
        covar[j * block : (j + 1) * block, i * block : (i + 1) * block] = value.T
        return 2.0 * (value * value)

    for core in (0, 1):
        a, b, c = 2 * core, 2 * core + 1, 2 - 2 * core
        squares += put(a, a, core, 0)
        squares += put(a, b, core, 1)
        squares += put(b, b, core, 2)
        squares += put(b, c, core, 3)
        squares += put(core, 2 + core, core, 4)

    cscale = jnp.sqrt(jnp.sum(squares, keepdims=True) + 1e-06)
    y = covar[...] * (1.0 / cscale)
    eye = (
        lax.broadcasted_iota(jnp.int32, (rows, rows), 0)
        == lax.broadcasted_iota(jnp.int32, (rows, rows), 1)
    ).astype(F32)
    yb = y.astype(BF)
    square = nn(yb, yb)
    squared = square.astype(BF)
    rest = -2.4375 * y + 1.6875 * square
    rest += nn(squared, (0.0625 * square - 0.5625 * y).astype(BF))
    restb = rest.astype(BF)
    left = 2.25 * y + nn(yb, restb)
    right = 4.5 * rest + nn(restb, restb)
    z3 = 3.375 * eye + 1.5 * rest - 0.5 * (
        5.0625 * left + nn(left.astype(BF), right.astype(BF))
    )
    out_ref[...] = (z3 * lax.rsqrt(cscale)).astype(BF)


def step(weights, blocks):
    low = weights.astype(BF)
    bents = [jnp.tanh(nn(low, block)) for block in blocks]
    pulled = nt(bents[0].astype(BF), blocks[0])
    slopes = 1.0 - bents[0] * bents[0]
    for bent, block in zip(bents[1:], blocks[1:]):
        pulled += nt(bent.astype(BF), block)
        slopes += 1.0 - bent * bent
    return pulled, jnp.sum(slopes, axis=1, keepdims=True)


def apply_kernel(part, whiten_ref, *refs):
    blocks, (weights_ref, white_ref, total_ref, slope_ref) = refs[:4], refs[-4:]
    weights = weights_ref[...]
    whites = [nn(whiten_ref[...], block[...]).astype(BF) for block in blocks]
    for k, white in enumerate(whites):
        white_ref[k] = white
    total, slope = step(weights, whites)
    if part:
        slope += refs[5][...]
        total += refs[4][...] - slope * weights
    total_ref[...] = total
    slope_ref[...] = slope


def decor_kernel(last, at, mine_ref, other_ref, *refs):
    whites, outs, (newer, lower, white, sem) = refs[:2], refs[2:-4], refs[-4:]
    count = mine_ref.shape[1]
    low, ax, ay = at[0], at[1], at[2]
    chunks = white.shape[0]
    first = 3 if last else 4
    copies = [
        pltpu.make_async_copy(
            ref.at[pl.ds(0, size)], white.at[pl.ds(start, size)], sem.at[k]
        )
        for k, (ref, start, size) in enumerate(
            zip(whites, (0, first), (first, chunks - first))
        )
    ]
    for copy in copies:
        copy.start()
    for k in range(4):
        i, j = ax ^ (k >> 1), ay ^ (k & 1)
        for ref, core in ((mine_ref, low), (other_ref, 1 - low)):
            start = pl.multiple_of((4 * i + 2 * core + j) * count, count)
            lower[pl.ds(start, count), :] = ref[k]

    raw = lower[...]
    gram = nt(raw, raw)
    gscale = jnp.sqrt(jnp.sum(gram * gram, keepdims=True) + 1e-06)
    value = 1.5 * raw.astype(F32) - (0.5 / gscale) * nn(gram.astype(BF), raw)
    value = value * lax.rsqrt(gscale)
    raw = value.astype(BF)
    gram = nt(raw, raw).astype(BF)
    newer[...] = 1.5 * value - 0.5 * nn(gram, raw)
    lower[...] = newer[...].astype(BF)
    start = pl.multiple_of((4 * ax + 2 * low) * count, count)
    size = 2 * count
    if not last:
        start = pl.multiple_of(start + ay * count, count)
        size = count
    raw = lower[...]
    gram = nt(lower[pl.ds(start, size), :], raw).astype(BF)
    weights = 1.5 * newer[pl.ds(start, size), :] - 0.5 * nn(gram, raw)
    for copy in copies:
        copy.wait()
    if last:
        outs[0][...] = weights
        width = white.shape[2]
        for k in range(chunks):
            place = 2 * (ax ^ (k >> 1)) + (low ^ (k & 1))
            outs[1][:, pl.ds(pl.multiple_of(place * width, width), width)] = nn(
                weights.astype(BF), white[k]
            ).astype(BF)
    else:
        total, slope = step(weights, [white[k] for k in range(chunks)])
        outs[0][...] = total - slope * weights


def shards(data, projection, initial):
    comps = lax.axis_size("comp")
    voxels = data.shape[1] * lax.axis_size("vox")
    vox, comp = lax.axis_index("vox"), lax.axis_index("comp")
    index = vox * comps + comp
    all_bits = (lax.axis_size("vox") * comps).bit_length() - 1
    low, across, near = 1, 2, comps
    far = [1 << k for k in range(near.bit_length(), all_bits)]
    at = jnp.stack([comp & 1, comp >> 1, vox & 1]).astype(jnp.int32)
    rows = projection.shape[0]
    size = data.shape[1] // comps

    mate = flip(projection, low)

    def columns(x, core):
        return lax.dynamic_slice_in_dim(data, (x * 2 + core) * size, size, 1)

    here, away = at[1], 1 - at[1]
    other = [columns(x, 1 - at[0]) for x in (away, here)]
    mine = [columns(x, at[0]) for x in (away, here)]
    other = [flip(block, low) for block in other]
    sent, kept = (
        run(
            project_kernel,
            shape((rows, size), kind),
            (projection, mine[k], mate, other[k]),
            specs=[VMEM] * 4,
        )
        for k, kind in enumerate((BF, F32))
    )
    reduced = (kept + flip(sent, across).astype(F32)).astype(BF)

    block = rows // 4
    piece = 5 * block // 4
    small = shape((piece, block), BF)
    there = flip(reduced, low)
    own, by, bx, bxy = run(
        covar_kernel,
        (shape((piece, block), F32), small, small, small),
        (at, reduced, there),
        scratch=[pltpu.VMEM((5 * block, block), F32)],
    )
    own, reduced = lax.optimization_barrier((own, reduced))
    at_x, at_y = flip(reduced, across), flip(reduced, near)
    own = own + flip(bxy, across | near).astype(F32)
    own = own + flip(bx, across).astype(F32)
    own = own + flip(by, near).astype(F32)
    own, reduced = lax.optimization_barrier((own, reduced))
    at_xy = flip(reduced, across | near)
    packed, at_x, at_y = sum_over(own, far, (at_x, at_y))
    packed, at_xy = spread(packed, across, near, (at_xy,))
    mate = flip(packed, low)
    whiten = run(
        functools.partial(whiten_kernel, voxels),
        shape((rows, rows), BF),
        (at, packed, mate),
        scratch=[pltpu.VMEM((2, 5 * block, block), F32), pltpu.VMEM((rows, rows), F32)],
    )

    count = initial.shape[0] // 2
    weights = lax.dynamic_slice_in_dim(initial, at[2] * count, count, 0)
    outs = (
        shape((4, rows, size), BF),
        shape((count, rows), F32),
        shape((count, 1), F32),
    )
    blocks = (reduced, there, at_x, at_y)
    white_here, total, slope = run(
        functools.partial(apply_kernel, False),
        outs,
        (whiten, *blocks, weights),
        specs=[VMEM] * 6,
    )
    blocks = (flip(at_x, low), flip(at_y, low), at_xy, flip(at_xy, low))
    white_there, newer, _ = run(
        functools.partial(apply_kernel, True),
        outs,
        (whiten, *blocks, total, slope, weights),
        specs=[VMEM] * 8,
    )
    whites = (white_here, white_there)

    for turn in range(ICA_ITERS):
        last = turn == ICA_ITERS - 1
        (stacked,) = spread(*sum_over(newer, far), across, near)
        chunks = 4 if last else 8
        outs = (
            (shape((2 * count, rows), F32), shape((2 * count, data.shape[1]), BF))
            if last
            else shape((count, rows), F32)
        )
        newer = run(
            functools.partial(decor_kernel, last),
            outs,
            (at, stacked, flip(stacked, low), *whites),
            specs=[SMEM, VMEM, VMEM] + [HBM] * 2,
            scratch=[
                pltpu.VMEM((rows, rows), F32),
                pltpu.VMEM((rows, rows), BF),
                pltpu.VMEM((chunks, rows, size), BF),
                pltpu.SemaphoreType.DMA((2,)),
            ],
        )
    return newer


def solution(mesh):
    return jax.shard_map(
        shards,
        mesh=mesh,
        in_specs=(P("comp", "vox"), P(None, "comp"), P("comp", None)),
        out_specs=(P("comp", None), P("comp", "vox")),
        check_vma=False,
    )
```

```python
import functools

import jax
import jax.numpy as jnp
from jax import lax
from jax.experimental import pallas as pl
from jax.experimental.pallas import tpu as pltpu
from jax.sharding import PartitionSpec as P

ICA_ITERS = 2
AXES = ("vox", "comp")
BF = jnp.bfloat16
F32 = jnp.float32
MIB = 1 << 20


def nn(left, right):
    return jnp.dot(left, right, preferred_element_type=F32)


def nt(left, right):
    return lax.dot_general(
        left, right, (((1,), (1,)), ((), ())), preferred_element_type=F32
    )


def rounded(x):
    return lax.reduce_precision(x, 8, 7)


def flip(x, mask):
    count = lax.axis_size("vox") * lax.axis_size("comp")
    return lax.ppermute(x, AXES, [(i, i ^ mask) for i in range(count)])


def sum_over(x, masks, due=()):
    for k in range(0, len(masks), 2):
        sent = x.astype(BF)
        first = flip(sent, masks[k])
        if k == 0:
            first, *due = lax.optimization_barrier((first, *due))
        x = rounded(x) + first.astype(F32)
        if k + 1 < len(masks):
            x = x + (
                flip(sent, masks[k + 1]).astype(F32)
                + flip(sent, masks[k] | masks[k + 1]).astype(F32)
            )
    return (x.astype(BF), *due)


def spread(x, across, near, due=()):
    both = flip(x, across | near)
    both, *due = lax.optimization_barrier((both, *due))
    return (jnp.stack([x, flip(x, near), flip(x, across), both]), *due)


VMEM = pl.BlockSpec(memory_space=pltpu.VMEM)
SMEM = pl.BlockSpec(memory_space=pltpu.SMEM)
HBM = pl.BlockSpec(memory_space=pltpu.HBM)


def run(kernel, outs, args, specs=None, scratch=(), limit=24):
    return pl.pallas_call(
        kernel,
        out_shape=outs,
        in_specs=specs or [SMEM] + [VMEM] * (len(args) - 1),
        out_specs=jax.tree.map(lambda _: VMEM, outs),
        scratch_shapes=list(scratch),
        compiler_params=pltpu.CompilerParams(vmem_limit_bytes=limit * MIB),
    )(*args)


def shape(dims, dtype):
    return jax.ShapeDtypeStruct(dims, dtype)


def project_kernel(left_ref, right_ref, mate_left_ref, mate_right_ref, out_ref):
    total = nn(left_ref[...], right_ref[...])
    total += nn(mate_left_ref[...], mate_right_ref[...])
    out_ref[...] = total.astype(out_ref.dtype)


def covar_kernel(at, here_ref, there_ref, own_ref, y_ref, x_ref, xy_ref, pack):
    rows = here_ref.shape[0]
    block = rows // 4

    def product(i, j, count):
        total = 0.0
        for ref in (here_ref, there_ref):
            left = ref[pl.ds(pl.multiple_of(i * block, block), count * block), :]
            right = ref[pl.ds(pl.multiple_of(j * block, block), 2 * block), :]
            total += nt(left, right)
        return total

    low = at[0]
    corner = product(2 * low, 2 * low, 2)
    cross = product(2 + low, 0, 1)
    pack[0 * block : 1 * block] = corner[:block, :block]
    pack[1 * block : 2 * block] = corner[:block, block:]
    pack[2 * block : 3 * block] = corner[block:, block:]
    pack[3 * block : 4 * block] = cross[:, :block]
    pack[4 * block : 5 * block] = cross[:, block:]
    piece = own_ref.shape[0]

    def quarter(i, j):
        return pack[pl.ds(pl.multiple_of((2 * i + j) * piece, piece), piece), :]

    ax, ay = at[1], at[2]
    own_ref[...] = quarter(ax, ay)
    y_ref[...] = quarter(ax, 1 - ay).astype(BF)
    x_ref[...] = quarter(1 - ax, ay).astype(BF)
    xy_ref[...] = quarter(1 - ax, 1 - ay).astype(BF)


def whiten_kernel(voxels, at, mine_ref, other_ref, out_ref, packs, covar):
    piece = mine_ref.shape[1]
    block = mine_ref.shape[2]
    rows = covar.shape[0]
    low, ax, ay = at[0], at[1], at[2]
    for k in range(4):
        i, j = ax ^ (k >> 1), ay ^ (k & 1)
        place = pl.ds(pl.multiple_of((2 * i + j) * piece, piece), piece)
        packs[low, place, :] = mine_ref[k].astype(F32) * (1.0 / voxels)
        packs[1 - low, place, :] = other_ref[k].astype(F32) * (1.0 / voxels)

    squares = jnp.zeros((block, block), F32)

    def put(i, j, core, k):
        value = packs[core, k * block : (k + 1) * block, :]
        covar[i * block : (i + 1) * block, j * block : (j + 1) * block] = value
        if i == j:
            return value * value
        covar[j * block : (j + 1) * block, i * block : (i + 1) * block] = value.T
        return 2.0 * (value * value)

    for core in (0, 1):
        squares += put(2 * core, 2 * core, core, 0)
        squares += put(2 * core, 2 * core + 1, core, 1)
        squares += put(2 * core + 1, 2 * core + 1, core, 2)
        squares += put(2 + core, 0, core, 3)
        squares += put(2 + core, 1, core, 4)

    cscale = jnp.sqrt(jnp.sum(squares, keepdims=True) + 1e-06)
    y = covar[...] * (1.0 / cscale)
    eye = (
        lax.broadcasted_iota(jnp.int32, (rows, rows), 0)
        == lax.broadcasted_iota(jnp.int32, (rows, rows), 1)
    ).astype(F32)
    yb = y.astype(BF)
    square = nn(yb, yb)
    squared = square.astype(BF)
    rest = -2.4375 * y + 1.6875 * square
    rest += nn(squared, (0.0625 * square - 0.5625 * y).astype(BF))
    restb = rest.astype(BF)
    left = 2.25 * y + nn(yb, restb)
    right = 4.5 * rest + nn(restb, restb)
    z3 = 3.375 * eye + 1.5 * rest - 0.5 * (
        5.0625 * left + nn(left.astype(BF), right.astype(BF))
    )
    out_ref[...] = (z3 * lax.rsqrt(cscale)).astype(BF)


def step(weights, blocks):
    low = weights.astype(BF)
    bents = [jnp.tanh(nn(low, block)) for block in blocks]
    pulled = nt(bents[0].astype(BF), blocks[0])
    slopes = 1.0 - bents[0] * bents[0]
    for bent, block in zip(bents[1:], blocks[1:]):
        pulled += nt(bent.astype(BF), block)
        slopes += 1.0 - bent * bent
    return pulled, jnp.sum(slopes, axis=1, keepdims=True)


def apply_kernel(whiten_ref, *refs):
    blocks, (weights_ref, white_ref, newer_ref) = refs[:-3], refs[-3:]
    weights = weights_ref[...]
    whites = []
    for k, block in enumerate(blocks):
        whites.append(nn(whiten_ref[...], block[...]).astype(BF))
        white_ref[k] = whites[k]
    total, slope = step(weights, whites)
    newer_ref[...] = total - slope * weights


def decor_kernel(last, at, mine_ref, other_ref, white_ref, *refs):
    outs, (newer, lower, white, sem) = refs[:-4], refs[-4:]
    count = mine_ref.shape[1]
    low, ax, ay = at[0], at[1], at[2]
    chunks = white.shape[0]
    copy = pltpu.make_async_copy(white_ref.at[pl.ds(0, chunks)], white, sem)
    copy.start()
    for k in range(4):
        i, j = ax ^ (k >> 1), ay ^ (k & 1)
        for ref, core in ((mine_ref, low), (other_ref, 1 - low)):
            start = pl.multiple_of((4 * i + 2 * core + j) * count, count)
            lower[pl.ds(start, count), :] = ref[k]

    raw = lower[...]
    gram = nt(raw, raw)
    gscale = jnp.sqrt(jnp.sum(gram * gram, keepdims=True) + 1e-06)
    value = 1.5 * raw.astype(F32) - (0.5 / gscale) * nn(gram.astype(BF), raw)
    value = value * lax.rsqrt(gscale)
    raw = value.astype(BF)
    gram = nt(raw, raw).astype(BF)
    newer[...] = 1.5 * value - 0.5 * nn(gram, raw)
    lower[...] = newer[...].astype(BF)
    start = pl.multiple_of((4 * ax + 2 * low) * count, count)
    size = 2 * count
    if not last:
        start = pl.multiple_of(start + ay * count, count)
        size = count
    raw = lower[...]
    gram = nt(lower[pl.ds(start, size), :], raw).astype(BF)
    weights = 1.5 * newer[pl.ds(start, size), :] - 0.5 * nn(gram, raw)
    copy.wait()
    if last:
        outs[0][...] = weights
        width = white.shape[2]
        for k in range(chunks):
            place = 2 * (ax ^ (k >> 1)) + (low ^ (k & 1))
            outs[1][:, pl.ds(pl.multiple_of(place * width, width), width)] = nn(
                weights.astype(BF), white[k]
            ).astype(BF)
    else:
        total, slope = step(weights, [white[k] for k in range(chunks)])
        outs[0][...] = total - slope * weights


def shards(data, projection, initial):
    comps = lax.axis_size("comp")
    voxels = data.shape[1] * lax.axis_size("vox")
    vox, comp = lax.axis_index("vox"), lax.axis_index("comp")
    index = vox * comps + comp
    all_bits = (lax.axis_size("vox") * comps).bit_length() - 1
    low, across, near = 1, 2, comps
    far = [1 << k for k in range(near.bit_length(), all_bits)]
    at = jnp.stack([comp & 1, comp >> 1, vox & 1]).astype(jnp.int32)
    rows = projection.shape[0]
    size = data.shape[1] // comps

    mate = flip(projection, low)

    def columns(x, core):
        return lax.dynamic_slice_in_dim(data, (x * 2 + core) * size, size, 1)

    here, away = at[1], 1 - at[1]
    other = [columns(x, 1 - at[0]) for x in (away, here)]
    mine = [columns(x, at[0]) for x in (away, here)]
    other = [flip(block, low) for block in other]
    sent, kept = (
        run(
            project_kernel,
            shape((rows, size), kind),
            (projection, mine[k], mate, other[k]),
            specs=[VMEM] * 4,
        )
        for k, kind in enumerate((BF, F32))
    )
    reduced = (kept + flip(sent, across).astype(F32)).astype(BF)

    block = rows // 4
    piece = 5 * block // 4
    small = shape((piece, block), BF)
    there = flip(reduced, low)
    own, by, bx, bxy = run(
        covar_kernel,
        (shape((piece, block), F32), small, small, small),
        (at, reduced, there),
        scratch=[pltpu.VMEM((5 * block, block), F32)],
    )
    own, reduced = lax.optimization_barrier((own, reduced))
    at_x, at_y = flip(reduced, across), flip(reduced, near)
    own = own + flip(bxy, across | near).astype(F32)
    own = own + flip(bx, across).astype(F32)
    own = own + flip(by, near).astype(F32)
    own, reduced = lax.optimization_barrier((own, reduced))
    at_xy = flip(reduced, across | near)
    packed, at_x, at_y = sum_over(own, far, (at_x, at_y))
    packed, at_xy = spread(packed, across, near, (at_xy,))
    mate = flip(packed, low)
    whiten = run(
        functools.partial(whiten_kernel, voxels),
        shape((rows, rows), BF),
        (at, packed, mate),
        scratch=[pltpu.VMEM((2, 5 * block, block), F32), pltpu.VMEM((rows, rows), F32)],
    )

    count = initial.shape[0] // 2
    weights = lax.dynamic_slice_in_dim(initial, at[2] * count, count, 0)
    blocks = (reduced, there, at_x, flip(at_x, low))
    blocks += (at_y, flip(at_y, low), at_xy, flip(at_xy, low))
    white, newer = run(
        apply_kernel,
        (shape((len(blocks), rows, size), BF), shape((count, rows), F32)),
        (whiten, *blocks, weights),
        specs=[VMEM] * (len(blocks) + 2),
    )

    for turn in range(ICA_ITERS):
        last = turn == ICA_ITERS - 1
        (stacked,) = spread(*sum_over(newer, far), across, near)
        chunks = len(blocks) // 2 if last else len(blocks)
        outs = (
            (shape((2 * count, rows), F32), shape((2 * count, data.shape[1]), BF))
            if last
            else shape((count, rows), F32)
        )
        newer = run(
            functools.partial(decor_kernel, last),
            outs,
            (at, stacked, flip(stacked, low), white),
            specs=[SMEM, VMEM, VMEM] + [HBM],
            scratch=[
                pltpu.VMEM((rows, rows), F32),
                pltpu.VMEM((rows, rows), BF),
                pltpu.VMEM((chunks, rows, size), BF),
                pltpu.SemaphoreType.DMA,
            ],
        )
    return newer


def solution(mesh):
    return jax.shard_map(
        shards,
        mesh=mesh,
        in_specs=(P("comp", "vox"), P(None, "comp"), P("comp", None)),
        out_specs=(P("comp", None), P("comp", "vox")),
        check_vma=False,
    )
```

```python
import functools

import jax
import jax.numpy as jnp
from jax import lax
from jax.experimental import pallas as pl
from jax.experimental.pallas import tpu as pltpu
from jax.sharding import PartitionSpec as P

ICA_ITERS = 2
AXES = ("vox", "comp")
BF = jnp.bfloat16
F32 = jnp.float32
MIB = 1 << 20


def place():
    vox, comp = lax.axis_index("vox"), lax.axis_index("comp")
    return lax.rem(comp, 2), lax.div(comp, 2), lax.rem(vox, 2)


def other(bit, flipped):
    return 1 - bit if flipped else bit


def nn(left, right):
    return jnp.dot(left, right, preferred_element_type=F32)


def nt(left, right):
    return lax.dot_general(
        left, right, (((1,), (1,)), ((), ())), preferred_element_type=F32
    )


def rounded(x):
    return lax.reduce_precision(x, 8, 7)


def flip(x, mask):
    count = lax.axis_size("vox") * lax.axis_size("comp")
    return lax.ppermute(x, AXES, [(i, i ^ mask) for i in range(count)])


def sum_over(x, masks, due=()):
    for k in range(0, len(masks), 2):
        sent = x.astype(BF)
        x = rounded(x) + flip(sent, masks[k]).astype(F32)
        if k + 1 < len(masks):
            both = flip(sent, masks[k] | masks[k + 1])
            if k == 0:
                both, *due = lax.optimization_barrier((both, *due))
            x = x + (flip(sent, masks[k + 1]).astype(F32) + both.astype(F32))
    return (x.astype(BF), *due)


def spread(x, across, near, due=()):
    both = flip(x, across | near)
    both, *due = lax.optimization_barrier((both, *due))
    blocks = [x, flip(x, near), flip(x, across), both]
    if due:
        mates = flip(jnp.stack(blocks), 1)
        return (blocks + [mates[k] for k in range(4)], *due)
    return blocks + [flip(block, 1) for block in blocks]


VMEM = pl.BlockSpec(memory_space=pltpu.VMEM)
HBM = pl.BlockSpec(memory_space=pltpu.HBM)


def run(kernel, outs, args, specs=None, out_spec=VMEM, scratch=(), limit=24):
    return pl.pallas_call(
        kernel,
        out_shape=outs,
        in_specs=specs or [VMEM] * len(args),
        out_specs=jax.tree.map(lambda _: out_spec, outs),
        scratch_shapes=list(scratch),
        compiler_params=pltpu.CompilerParams(vmem_limit_bytes=limit * MIB),
    )(*args)


def shape(dims, dtype):
    return jax.ShapeDtypeStruct(dims, dtype)


def project_kernel(left_ref, right_ref, mate_left_ref, mate_right_ref, out_ref):
    total = nn(left_ref[...], right_ref[...])
    total += nn(mate_left_ref[...], mate_right_ref[...])
    out_ref[...] = total.astype(out_ref.dtype)


def covar_kernel(here_ref, there_ref, own_ref, y_ref, x_ref, xy_ref, pack):
    rows = here_ref.shape[0]
    block = rows // 4

    def product(i, j, count):
        total = 0.0
        for ref in (here_ref, there_ref):
            left = ref[pl.ds(pl.multiple_of(i * block, block), count * block), :]
            right = ref[pl.ds(pl.multiple_of(j * block, block), 2 * block), :]
            total += nt(left, right)
        return total

    low, ax, ay = place()
    corner = product(2 * low, 2 * low, 2)
    cross = product(2 + low, 0, 1)
    pack[0 * block : 1 * block] = corner[:block, :block]
    pack[1 * block : 2 * block] = corner[:block, block:]
    pack[2 * block : 3 * block] = corner[block:, block:]
    pack[3 * block : 4 * block] = cross[:, :block]
    pack[4 * block : 5 * block] = cross[:, block:]
    piece = own_ref.shape[0]

    def quarter(i, j):
        return pack[pl.ds(pl.multiple_of((2 * i + j) * piece, piece), piece), :]

    own_ref[...] = quarter(ax, ay)
    y_ref[...] = quarter(ax, 1 - ay).astype(BF)
    x_ref[...] = quarter(1 - ax, ay).astype(BF)
    xy_ref[...] = quarter(1 - ax, 1 - ay).astype(BF)


def whiten_kernel(voxels, *refs):
    mine, mates, (out_ref, packs, covar) = refs[:4], refs[4:8], refs[8:]
    piece, block = mine[0].shape
    rows = covar.shape[0]
    low, ax, ay = place()
    for k in range(4):
        spot = 2 * other(ax, k & 2) + other(ay, k & 1)
        spot = pl.ds(pl.multiple_of(spot * piece, piece), piece)
        packs[low, spot, :] = mine[k][...].astype(F32) * (1.0 / voxels)
        packs[1 - low, spot, :] = mates[k][...].astype(F32) * (1.0 / voxels)

    squares = jnp.zeros((block, block), F32)

    def put(i, j, core, k):
        value = packs[core, k * block : (k + 1) * block, :]
        covar[i * block : (i + 1) * block, j * block : (j + 1) * block] = value
        if i == j:
            return value * value
        covar[j * block : (j + 1) * block, i * block : (i + 1) * block] = value.T
        return 2.0 * (value * value)

    for core in (0, 1):
        squares += put(2 * core, 2 * core, core, 0)
        squares += put(2 * core, 2 * core + 1, core, 1)
        squares += put(2 * core + 1, 2 * core + 1, core, 2)
        squares += put(2 + core, 0, core, 3)
        squares += put(2 + core, 1, core, 4)

    cscale = jnp.sqrt(jnp.sum(squares, keepdims=True) + 1e-06)
    y = covar[...] * (1.0 / cscale)
    eye = (
        lax.broadcasted_iota(jnp.int32, (rows, rows), 0)
        == lax.broadcasted_iota(jnp.int32, (rows, rows), 1)
    ).astype(F32)
    yb = y.astype(BF)
    square = nn(yb, yb)
    squared = square.astype(BF)
    rest = -2.4375 * y + 1.6875 * square
    rest += nn(squared, (0.0625 * square - 0.5625 * y).astype(BF))
    restb = rest.astype(BF)
    left = 2.25 * y + nn(yb, restb)
    right = 4.5 * rest + nn(restb, restb)
    z3 = 3.375 * eye + 1.5 * rest - 0.5 * (
        5.0625 * left + nn(left.astype(BF), right.astype(BF))
    )
    out_ref[...] = (z3 * lax.rsqrt(cscale)).astype(BF)


def step(weights, blocks):
    low = weights.astype(BF)
    bents = [jnp.tanh(nn(low, block)) for block in blocks]
    pulled = nt(bents[0].astype(BF), blocks[0])
    slopes = 1.0 - bents[0] * bents[0]
    for bent, block in zip(bents[1:], blocks[1:]):
        pulled += nt(bent.astype(BF), block)
        slopes += 1.0 - bent * bent
    return pulled, jnp.sum(slopes, axis=1, keepdims=True)


def apply_kernel(whiten_ref, *refs):
    blocks, (weights_ref, white_ref, newer_ref) = refs[:-3], refs[-3:]
    weights = weights_ref[...]
    whites = []
    for k, block in enumerate(blocks):
        whites.append(nn(whiten_ref[...], block[...]).astype(BF))
        white_ref[k] = whites[k]
    total, slope = step(weights, whites)
    newer_ref[...] = total - slope * weights


def decor_kernel(last, *refs):
    mine, mates, white_ref = refs[:4], refs[4:8], refs[8]
    outs, scratch = (refs[9:11], refs[11:]) if last else (refs[9:10], refs[10:])
    newer, lower, white, sem, *held = scratch
    count = mine[0].shape[0]
    low, ax, ay = place()
    chunks = white.shape[0]
    copy = pltpu.make_async_copy(white_ref.at[pl.ds(0, chunks)], white, sem)
    copy.start()
    for k in range(4):
        spot = 4 * other(ax, k & 2) + other(ay, k & 1)
        for ref, core in ((mine[k], low), (mates[k], 1 - low)):
            start = pl.multiple_of((spot + 2 * core) * count, count)
            lower[pl.ds(start, count), :] = ref[...]

    raw = lower[...]
    gram = nt(raw, raw)
    gscale = jnp.sqrt(jnp.sum(gram * gram, keepdims=True) + 1e-06)
    value = 1.5 * raw.astype(F32) - (0.5 / gscale) * nn(gram.astype(BF), raw)
    value = value * lax.rsqrt(gscale)
    raw = value.astype(BF)
    gram = nt(raw, raw).astype(BF)
    newer[...] = 1.5 * value - 0.5 * nn(gram, raw)
    lower[...] = newer[...].astype(BF)
    start = pl.multiple_of((4 * ax + 2 * low) * count, count)
    size = 2 * count
    if not last:
        start = pl.multiple_of(start + ay * count, count)
        size = count
    raw = lower[...]
    gram = nt(lower[pl.ds(start, size), :], raw).astype(BF)
    weights = 1.5 * newer[pl.ds(start, size), :] - 0.5 * nn(gram, raw)
    copy.wait()
    if last:
        unmixing, sources, sems = held
        unmixing[...] = weights
        copies = [pltpu.make_async_copy(unmixing, outs[0], sems.at[chunks])]
        copies[0].start()
        width = white.shape[2]
        for k in range(chunks):
            sources[k] = nn(weights.astype(BF), white[k]).astype(BF)
            spot = 2 * other(ax, k & 2) + other(low, k & 1)
            spot = pl.ds(pl.multiple_of(spot * width, width), width)
            copies.append(
                pltpu.make_async_copy(sources.at[k], outs[1].at[:, spot], sems.at[k])
            )
            copies[-1].start()
        for copy in copies:
            copy.wait()
    else:
        total, slope = step(weights, [white[k] for k in range(chunks)])
        outs[0][...] = total - slope * weights


def shards(data, projection, initial):
    comps = lax.axis_size("comp")
    voxels = data.shape[1] * lax.axis_size("vox")
    all_bits = (lax.axis_size("vox") * comps).bit_length() - 1
    low, across, near = 1, 2, comps
    far = [1 << k for k in range(near.bit_length(), all_bits)]
    core, far_x, near_y = place()
    rows = projection.shape[0]
    size = data.shape[1] // comps

    mate = flip(projection, low)

    def columns(x, core):
        return lax.dynamic_slice_in_dim(data, (x * 2 + core) * size, size, 1)

    sides = (1 - far_x, far_x)
    theirs = [flip(columns(x, 1 - core), low) for x in sides]
    mine = [columns(x, core) for x in sides]
    sent, kept = (
        run(
            project_kernel,
            shape((rows, size), kind),
            (projection, mine[k], mate, theirs[k]),
        )
        for k, kind in enumerate((BF, F32))
    )
    reduced = (kept + flip(sent, across).astype(F32)).astype(BF)

    block = rows // 4
    piece = 5 * block // 4
    small = shape((piece, block), BF)
    there = flip(reduced, low)
    own, by, bx, bxy = run(
        covar_kernel,
        (shape((piece, block), F32), small, small, small),
        (reduced, there),
        scratch=[pltpu.VMEM((5 * block, block), F32)],
    )
    own, reduced = lax.optimization_barrier((own, reduced))
    at_x, at_y = flip(reduced, across), flip(reduced, near)
    own = own + flip(bxy, across | near).astype(F32)
    own = own + flip(bx, across).astype(F32)
    own = own + flip(by, near).astype(F32)
    own, reduced = lax.optimization_barrier((own, reduced))
    at_xy = flip(reduced, across | near)
    packed, at_x, at_y = sum_over(own, far, (at_x, at_y))
    packed, at_xy = spread(packed, across, near, (at_xy,))
    whiten = run(
        functools.partial(whiten_kernel, voxels),
        shape((rows, rows), BF),
        packed,
        scratch=[pltpu.VMEM((2, 5 * block, block), F32), pltpu.VMEM((rows, rows), F32)],
    )

    count = initial.shape[0] // 2
    weights = lax.dynamic_slice_in_dim(initial, near_y * count, count, 0)
    blocks = (reduced, there, at_x, flip(at_x, low))
    blocks += (at_y, flip(at_y, low), at_xy, flip(at_xy, low))
    white, newer = run(
        apply_kernel,
        (shape((len(blocks), rows, size), BF), shape((count, rows), F32)),
        (whiten, *blocks, weights),
    )

    for turn in range(ICA_ITERS):
        last = turn == ICA_ITERS - 1
        stacked = spread(*sum_over(newer, far), across, near)
        chunks = len(blocks) // 2 if last else len(blocks)
        outs = (
            (shape((2 * count, rows), F32), shape((2 * count, data.shape[1]), BF))
            if last
            else shape((count, rows), F32)
        )
        scratch = [
            pltpu.VMEM((rows, rows), F32),
            pltpu.VMEM((rows, rows), BF),
            pltpu.VMEM((chunks, rows, size), BF),
            pltpu.SemaphoreType.DMA,
        ]
        if last:
            scratch += [
                pltpu.VMEM((2 * count, rows), F32),
                pltpu.VMEM((chunks, 2 * count, size), BF),
                pltpu.SemaphoreType.DMA((chunks + 1,)),
            ]
        newer = run(
            functools.partial(decor_kernel, last),
            outs,
            (*stacked, white),
            specs=[VMEM] * 8 + [HBM],
            out_spec=HBM if last else VMEM,
            scratch=scratch,
        )
    return newer


def solution(mesh):
    return jax.shard_map(
        shards,
        mesh=mesh,
        in_specs=(P("comp", "vox"), P(None, "comp"), P("comp", None)),
        out_specs=(P("comp", None), P("comp", "vox")),
        check_vma=False,
    )
```

```python
import functools

import jax
import jax.numpy as jnp
from jax import lax
from jax.experimental import pallas as pl
from jax.experimental.pallas import tpu as pltpu
from jax.sharding import PartitionSpec as P

ICA_ITERS = 2
AXES = ("vox", "comp")
BF = jnp.bfloat16
HALF = jnp.float16
F32 = jnp.float32
MIB = 1 << 20


def place():
    vox, comp = lax.axis_index("vox"), lax.axis_index("comp")
    return lax.rem(comp, 2), lax.div(comp, 2), lax.rem(vox, 2)


def other(bit, flipped):
    return 1 - bit if flipped else bit


def nn(left, right):
    return jnp.dot(left, right, preferred_element_type=F32)


def nt(left, right):
    return lax.dot_general(
        left, right, (((1,), (1,)), ((), ())), preferred_element_type=F32
    )


def rounded(x, kind):
    info = jnp.finfo(kind)
    return lax.reduce_precision(x, info.nexp, info.nmant)


def flip(x, mask):
    count = lax.axis_size("vox") * lax.axis_size("comp")
    return lax.ppermute(x, AXES, [(i, i ^ mask) for i in range(count)])


def sum_over(x, masks, kind, due=()):
    for k in range(0, len(masks), 2):
        sent = x.astype(kind)
        x = rounded(x, kind) + flip(sent, masks[k]).astype(F32)
        if k + 1 < len(masks):
            both = flip(sent, masks[k] | masks[k + 1])
            if k == 0:
                both, *due = lax.optimization_barrier((both, *due))
            x = x + (flip(sent, masks[k + 1]).astype(F32) + both.astype(F32))
    return (x.astype(kind), *due)


def spread(x, across, near, due=()):
    both = flip(x, across | near)
    both, *due = lax.optimization_barrier((both, *due))
    blocks = [x, flip(x, near), flip(x, across), both]
    if due:
        mates = flip(jnp.stack(blocks), 1)
        return (blocks + [mates[k] for k in range(4)], *due)
    return blocks + [flip(block, 1) for block in blocks]


VMEM = pl.BlockSpec(memory_space=pltpu.VMEM)
HBM = pl.BlockSpec(memory_space=pltpu.HBM)


def run(kernel, outs, args, specs=None, out_spec=VMEM, scratch=(), limit=24):
    return pl.pallas_call(
        kernel,
        out_shape=outs,
        in_specs=specs or [VMEM] * len(args),
        out_specs=jax.tree.map(lambda _: out_spec, outs),
        scratch_shapes=list(scratch),
        compiler_params=pltpu.CompilerParams(vmem_limit_bytes=limit * MIB),
    )(*args)


def shape(dims, dtype):
    return jax.ShapeDtypeStruct(dims, dtype)


def sent_kernel(left_ref, right_ref, mate_left_ref, mate_right_ref, out_ref):
    total = nn(left_ref[...], right_ref[...])
    total += nn(mate_left_ref[...], mate_right_ref[...])
    rows = total.shape[0]
    most = jnp.max(jnp.abs(total), axis=0, keepdims=True)
    power = jnp.floor(jnp.log2(jnp.maximum(most, 1e-30))) - 14.0
    out_ref[:rows] = total * jnp.exp2(-power)
    out_ref[rows:] = jnp.broadcast_to(power, (out_ref.shape[0] - rows, total.shape[1]))


def project_kernel(left_ref, right_ref, mate_left_ref, mate_right_ref, out_ref):
    total = nn(left_ref[...], right_ref[...])
    total += nn(mate_left_ref[...], mate_right_ref[...])
    out_ref[...] = total.astype(out_ref.dtype)


def covar_kernel(here_ref, there_ref, own_ref, y_ref, x_ref, xy_ref, pack):
    rows = here_ref.shape[0]
    block = rows // 4

    def product(i, j, count):
        total = 0.0
        for ref in (here_ref, there_ref):
            left = ref[pl.ds(pl.multiple_of(i * block, block), count * block), :]
            right = ref[pl.ds(pl.multiple_of(j * block, block), 2 * block), :]
            total += nt(left, right)
        return total

    low, ax, ay = place()
    corner = product(2 * low, 2 * low, 2)
    cross = product(2 + low, 0, 1)
    pack[0 * block : 1 * block] = corner[:block, :block]
    pack[1 * block : 2 * block] = corner[:block, block:]
    pack[2 * block : 3 * block] = corner[block:, block:]
    pack[3 * block : 4 * block] = cross[:, :block]
    pack[4 * block : 5 * block] = cross[:, block:]
    piece = own_ref.shape[0]

    def quarter(i, j):
        return pack[pl.ds(pl.multiple_of((2 * i + j) * piece, piece), piece), :]

    own_ref[...] = quarter(ax, ay)
    y_ref[...] = quarter(ax, 1 - ay).astype(BF)
    x_ref[...] = quarter(1 - ax, ay).astype(BF)
    xy_ref[...] = quarter(1 - ax, 1 - ay).astype(BF)


def whiten_kernel(voxels, *refs):
    mine, mates, (out_ref, packs, covar) = refs[:4], refs[4:8], refs[8:]
    piece, block = mine[0].shape
    rows = covar.shape[0]
    low, ax, ay = place()
    for k in range(4):
        spot = 2 * other(ax, k & 2) + other(ay, k & 1)
        spot = pl.ds(pl.multiple_of(spot * piece, piece), piece)
        packs[low, spot, :] = mine[k][...].astype(F32) * (1.0 / voxels)
        packs[1 - low, spot, :] = mates[k][...].astype(F32) * (1.0 / voxels)

    squares = jnp.zeros((block, block), F32)

    def put(i, j, core, k):
        value = packs[core, k * block : (k + 1) * block, :]
        covar[i * block : (i + 1) * block, j * block : (j + 1) * block] = value
        if i == j:
            return value * value
        covar[j * block : (j + 1) * block, i * block : (i + 1) * block] = value.T
        return 2.0 * (value * value)

    for core in (0, 1):
        squares += put(2 * core, 2 * core, core, 0)
        squares += put(2 * core, 2 * core + 1, core, 1)
        squares += put(2 * core + 1, 2 * core + 1, core, 2)
        squares += put(2 + core, 0, core, 3)
        squares += put(2 + core, 1, core, 4)

    cscale = jnp.sqrt(jnp.sum(squares, keepdims=True) + 1e-06)
    y = covar[...] * (1.0 / cscale)
    eye = (
        lax.broadcasted_iota(jnp.int32, (rows, rows), 0)
        == lax.broadcasted_iota(jnp.int32, (rows, rows), 1)
    ).astype(F32)
    yb = y.astype(BF)
    square = nn(yb, yb)
    squared = square.astype(BF)
    rest = -2.4375 * y + 1.6875 * square
    rest += nn(squared, (0.0625 * square - 0.5625 * y).astype(BF))
    restb = rest.astype(BF)
    left = 2.25 * y + nn(yb, restb)
    right = 4.5 * rest + nn(restb, restb)
    z3 = 3.375 * eye + 1.5 * rest - 0.5 * (
        5.0625 * left + nn(left.astype(BF), right.astype(BF))
    )
    out_ref[...] = (z3 * lax.rsqrt(cscale)).astype(BF)


def step(weights, blocks):
    low = weights.astype(BF)
    bents = [jnp.tanh(nn(low, block)) for block in blocks]
    pulled = nt(bents[0].astype(BF), blocks[0])
    slopes = 1.0 - bents[0] * bents[0]
    for bent, block in zip(bents[1:], blocks[1:]):
        pulled += nt(bent.astype(BF), block)
        slopes += 1.0 - bent * bent
    return pulled, jnp.sum(slopes, axis=1, keepdims=True)


def apply_kernel(scale, whiten_ref, *refs):
    blocks, (weights_ref, white_ref, newer_ref) = refs[:-3], refs[-3:]
    weights = weights_ref[...]
    whites = []
    for k, block in enumerate(blocks):
        whites.append(nn(whiten_ref[...], block[...]).astype(BF))
        white_ref[k] = whites[k]
    total, slope = step(weights, whites)
    newer_ref[...] = (total - slope * weights) * scale


def decor_kernel(last, scale, *refs):
    mine, mates, white_ref = refs[:4], refs[4:8], refs[8]
    outs, scratch = (refs[9:11], refs[11:]) if last else (refs[9:10], refs[10:])
    newer, lower, white, sem, *held = scratch
    count = mine[0].shape[0]
    low, ax, ay = place()
    chunks = white.shape[0]
    copy = pltpu.make_async_copy(white_ref.at[pl.ds(0, chunks)], white, sem)
    copy.start()
    for k in range(4):
        spot = 4 * other(ax, k & 2) + other(ay, k & 1)
        for ref, core in ((mine[k], low), (mates[k], 1 - low)):
            start = pl.multiple_of((spot + 2 * core) * count, count)
            newer[pl.ds(start, count), :] = ref[...]
            lower[pl.ds(start, count), :] = ref[...].astype(BF)

    raw = lower[...]
    gram = nt(raw, raw)
    gscale = jnp.sqrt(jnp.sum(gram * gram, keepdims=True) + 1e-06)
    value = 1.5 * newer[...] - (0.5 / gscale) * nn(gram.astype(BF), raw)
    value = value * lax.rsqrt(gscale)
    raw = value.astype(BF)
    gram = nt(raw, raw).astype(BF)
    newer[...] = 1.5 * value - 0.5 * nn(gram, raw)
    lower[...] = newer[...].astype(BF)
    start = pl.multiple_of((4 * ax + 2 * low) * count, count)
    size = 2 * count
    if not last:
        start = pl.multiple_of(start + ay * count, count)
        size = count
    raw = lower[...]
    gram = nt(lower[pl.ds(start, size), :], raw).astype(BF)
    weights = 1.5 * newer[pl.ds(start, size), :] - 0.5 * nn(gram, raw)
    copy.wait()
    if last:
        unmixing, sources, sems = held
        unmixing[...] = weights
        copies = [pltpu.make_async_copy(unmixing, outs[0], sems.at[chunks])]
        copies[0].start()
        width = white.shape[2]
        for k in range(chunks):
            sources[k] = nn(weights.astype(BF), white[k]).astype(BF)
            spot = 2 * other(ax, k & 2) + other(low, k & 1)
            spot = pl.ds(pl.multiple_of(spot * width, width), width)
            copies.append(
                pltpu.make_async_copy(sources.at[k], outs[1].at[:, spot], sems.at[k])
            )
            copies[-1].start()
        for copy in copies:
            copy.wait()
    else:
        total, slope = step(weights, [white[k] for k in range(chunks)])
        outs[0][...] = (total - slope * weights) * scale


def shards(data, projection, initial):
    comps = lax.axis_size("comp")
    voxels = data.shape[1] * lax.axis_size("vox")
    all_bits = (lax.axis_size("vox") * comps).bit_length() - 1
    low, across, near = 1, 2, comps
    far = [1 << k for k in range(near.bit_length(), all_bits)]
    core, far_x, near_y = place()
    rows = projection.shape[0]
    size = data.shape[1] // comps

    mate = flip(projection, low)

    def columns(x, core):
        return lax.dynamic_slice_in_dim(data, (x * 2 + core) * size, size, 1)

    sides = (1 - far_x, far_x)
    theirs = [flip(columns(x, 1 - core), low) for x in sides]
    mine = [columns(x, core) for x in sides]
    sent, kept = (
        run(kernel, shape((count, size), F32), (projection, mine[k], mate, theirs[k]))
        for k, (kernel, count) in enumerate(
            ((sent_kernel, rows + 16), (project_kernel, rows))
        )
    )
    sent = flip(sent.astype(HALF), across).astype(F32)
    reduced = (kept + sent[:rows] * jnp.exp2(sent[rows : rows + 1])).astype(BF)

    block = rows // 4
    piece = 5 * block // 4
    small = shape((piece, block), BF)
    there = flip(reduced, low)
    own, by, bx, bxy = run(
        covar_kernel,
        (shape((piece, block), F32), small, small, small),
        (reduced, there),
        scratch=[pltpu.VMEM((5 * block, block), F32)],
    )
    own, reduced = lax.optimization_barrier((own, reduced))
    at_x, at_y = flip(reduced, across), flip(reduced, near)
    own = own + flip(bxy, across | near).astype(F32)
    own = own + flip(bx, across).astype(F32)
    own = own + flip(by, near).astype(F32)
    own, reduced = lax.optimization_barrier((own, reduced))
    at_xy = flip(reduced, across | near)
    packed, at_x, at_y = sum_over(own, far, BF, (at_x, at_y))
    packed, at_xy = spread(packed, across, near, (at_xy,))
    whiten = run(
        functools.partial(whiten_kernel, voxels),
        shape((rows, rows), BF),
        packed,
        scratch=[pltpu.VMEM((2, 5 * block, block), F32), pltpu.VMEM((rows, rows), F32)],
    )

    count = initial.shape[0] // 2
    weights = lax.dynamic_slice_in_dim(initial, near_y * count, count, 0)
    scale = 8192.0 / voxels
    blocks = (reduced, there, at_x, flip(at_x, low))
    blocks += (at_y, flip(at_y, low), at_xy, flip(at_xy, low))
    white, newer = run(
        functools.partial(apply_kernel, scale),
        (shape((len(blocks), rows, size), BF), shape((count, rows), F32)),
        (whiten, *blocks, weights),
    )

    for turn in range(ICA_ITERS):
        last = turn == ICA_ITERS - 1
        stacked = spread(*sum_over(newer, far, HALF), across, near)
        stacked = [part.astype(F32) * (1.0 / scale) for part in stacked]
        chunks = len(blocks) // 2 if last else len(blocks)
        outs = (
            (shape((2 * count, rows), F32), shape((2 * count, data.shape[1]), BF))
            if last
            else shape((count, rows), F32)
        )
        scratch = [
            pltpu.VMEM((rows, rows), F32),
            pltpu.VMEM((rows, rows), BF),
            pltpu.VMEM((chunks, rows, size), BF),
            pltpu.SemaphoreType.DMA,
        ]
        if last:
            scratch += [
                pltpu.VMEM((2 * count, rows), F32),
                pltpu.VMEM((chunks, 2 * count, size), BF),
                pltpu.SemaphoreType.DMA((chunks + 1,)),
            ]
        newer = run(
            functools.partial(decor_kernel, last, scale),
            outs,
            (*stacked, white),
            specs=[VMEM] * 8 + [HBM],
            out_spec=HBM if last else VMEM,
            scratch=scratch,
        )
    return newer


def solution(mesh):
    return jax.shard_map(
        shards,
        mesh=mesh,
        in_specs=(P("comp", "vox"), P(None, "comp"), P("comp", None)),
        out_specs=(P("comp", None), P("comp", "vox")),
        check_vma=False,
    )
```

```python
import functools

import jax
import jax.numpy as jnp
from jax import lax
from jax.experimental import pallas as pl
from jax.experimental.pallas import tpu as pltpu
from jax.sharding import PartitionSpec as P

ICA_ITERS = 2
AXES = ("vox", "comp")
BF = jnp.bfloat16
HALF = jnp.float16
F32 = jnp.float32
MIB = 1 << 20


def place():
    vox, comp = lax.axis_index("vox"), lax.axis_index("comp")
    return lax.rem(comp, 2), lax.div(comp, 2), lax.rem(vox, 2)


def other(bit, flipped):
    return 1 - bit if flipped else bit


def nn(left, right):
    return jnp.dot(left, right, preferred_element_type=F32)


def nt(left, right):
    return lax.dot_general(
        left, right, (((1,), (1,)), ((), ())), preferred_element_type=F32
    )


def rounded(x, kind):
    info = jnp.finfo(kind)
    return lax.reduce_precision(x, info.nexp, info.nmant)


def flip(x, mask):
    count = lax.axis_size("vox") * lax.axis_size("comp")
    return lax.ppermute(x, AXES, [(i, i ^ mask) for i in range(count)])


def sum_over(x, masks, kind, due=()):
    for k in range(0, len(masks), 2):
        sent = x.astype(kind)
        x = rounded(x, kind) + flip(sent, masks[k]).astype(F32)
        if k + 1 < len(masks):
            both = flip(sent, masks[k] | masks[k + 1])
            if k == 0:
                both, *due = lax.optimization_barrier((both, *due))
            x = x + (flip(sent, masks[k + 1]).astype(F32) + both.astype(F32))
    return (x.astype(kind), *due)


def spread(x, across, near, due=()):
    both = flip(x, across | near)
    both, *due = lax.optimization_barrier((both, *due))
    blocks = [x, flip(x, near), flip(x, across), both]
    if due:
        mates = flip(jnp.stack(blocks), 1)
        return (blocks + [mates[k] for k in range(4)], *due)
    return blocks + [flip(block, 1) for block in blocks]


VMEM = pl.BlockSpec(memory_space=pltpu.VMEM)
HBM = pl.BlockSpec(memory_space=pltpu.HBM)


def run(kernel, outs, args, specs=None, out_spec=VMEM, scratch=(), cost=0):
    return pl.pallas_call(
        kernel,
        out_shape=outs,
        in_specs=specs or [VMEM] * len(args),
        out_specs=jax.tree.map(lambda _: out_spec, outs),
        scratch_shapes=list(scratch),
        compiler_params=pltpu.CompilerParams(vmem_limit_bytes=24 * MIB),
        cost_estimate=pl.CostEstimate(flops=cost, bytes_accessed=cost // 256, transcendentals=0)
        if cost
        else None,
    )(*args)


def shape(dims, dtype):
    return jax.ShapeDtypeStruct(dims, dtype)


def sent_kernel(left_ref, right_ref, mate_left_ref, mate_right_ref, out_ref):
    total = nn(left_ref[...], right_ref[...])
    total += nn(mate_left_ref[...], mate_right_ref[...])
    rows = total.shape[0]
    most = jnp.max(jnp.abs(total), axis=0, keepdims=True)
    power = jnp.floor(jnp.log2(jnp.maximum(most, 1e-30))) - 14.0
    out_ref[:rows] = total * jnp.exp2(-power)
    out_ref[rows:] = jnp.broadcast_to(power, (out_ref.shape[0] - rows, total.shape[1]))


def project_kernel(left_ref, right_ref, mate_left_ref, mate_right_ref, out_ref):
    total = nn(left_ref[...], right_ref[...])
    total += nn(mate_left_ref[...], mate_right_ref[...])
    out_ref[...] = total.astype(out_ref.dtype)


def covar_kernel(here_ref, there_ref, own_ref, y_ref, x_ref, xy_ref, pack):
    rows = here_ref.shape[0]
    block = rows // 4

    def product(i, j, count):
        total = 0.0
        for ref in (here_ref, there_ref):
            left = ref[pl.ds(pl.multiple_of(i * block, block), count * block), :]
            right = ref[pl.ds(pl.multiple_of(j * block, block), 2 * block), :]
            total += nt(left, right)
        return total

    low, ax, ay = place()
    corner = product(2 * low, 2 * low, 2)
    cross = product(2 + low, 0, 1)
    pack[0 * block : 1 * block] = corner[:block, :block]
    pack[1 * block : 2 * block] = corner[:block, block:]
    pack[2 * block : 3 * block] = corner[block:, block:]
    pack[3 * block : 4 * block] = cross[:, :block]
    pack[4 * block : 5 * block] = cross[:, block:]
    piece = own_ref.shape[0]

    def quarter(i, j):
        return pack[pl.ds(pl.multiple_of((2 * i + j) * piece, piece), piece), :]

    own_ref[...] = quarter(ax, ay)
    y_ref[...] = quarter(ax, 1 - ay).astype(BF)
    x_ref[...] = quarter(1 - ax, ay).astype(BF)
    xy_ref[...] = quarter(1 - ax, 1 - ay).astype(BF)


def whiten_kernel(voxels, *refs):
    mine, mates = refs[:4], refs[4:8]
    weights_ref, out_ref, mixed_ref, packs, covar = refs[8:]
    piece, block = mine[0].shape
    rows = covar.shape[0]
    low, ax, ay = place()
    for k in range(4):
        spot = 2 * other(ax, k & 2) + other(ay, k & 1)
        spot = pl.ds(pl.multiple_of(spot * piece, piece), piece)
        packs[low, spot, :] = mine[k][...].astype(F32) * (1.0 / voxels)
        packs[1 - low, spot, :] = mates[k][...].astype(F32) * (1.0 / voxels)

    squares = jnp.zeros((block, block), F32)

    def put(i, j, core, k):
        value = packs[core, k * block : (k + 1) * block, :]
        covar[i * block : (i + 1) * block, j * block : (j + 1) * block] = value
        if i == j:
            return value * value
        covar[j * block : (j + 1) * block, i * block : (i + 1) * block] = value.T
        return 2.0 * (value * value)

    for core in (0, 1):
        squares += put(2 * core, 2 * core, core, 0)
        squares += put(2 * core, 2 * core + 1, core, 1)
        squares += put(2 * core + 1, 2 * core + 1, core, 2)
        squares += put(2 + core, 0, core, 3)
        squares += put(2 + core, 1, core, 4)

    cscale = jnp.sqrt(jnp.sum(squares, keepdims=True) + 1e-06)
    y = covar[...] * (1.0 / cscale)
    eye = (
        lax.broadcasted_iota(jnp.int32, (rows, rows), 0)
        == lax.broadcasted_iota(jnp.int32, (rows, rows), 1)
    ).astype(F32)
    yb = y.astype(BF)
    square = nn(yb, yb)
    squared = square.astype(BF)
    rest = -2.4375 * y + 1.6875 * square
    rest += nn(squared, (0.0625 * square - 0.5625 * y).astype(BF))
    restb = rest.astype(BF)
    left = 2.25 * y + nn(yb, restb)
    right = 4.5 * rest + nn(restb, restb)
    z3 = 3.375 * eye + 1.5 * rest - 0.5 * (
        5.0625 * left + nn(left.astype(BF), right.astype(BF))
    )
    whiten = (z3 * lax.rsqrt(cscale)).astype(BF)
    out_ref[...] = whiten
    mixed_ref[...] = nn(weights_ref[...].astype(BF), whiten).astype(BF)


def step(weights, blocks):
    low = weights.astype(BF)
    bents = [jnp.tanh(nn(low, block)) for block in blocks]
    pulled = nt(bents[0].astype(BF), blocks[0])
    slopes = 1.0 - bents[0] * bents[0]
    for bent, block in zip(bents[1:], blocks[1:]):
        pulled += nt(bent.astype(BF), block)
        slopes += 1.0 - bent * bent
    return pulled, jnp.sum(slopes, axis=1, keepdims=True)


def apply_kernel(scale, mixed_ref, whiten_ref, weights_ref, *refs):
    blocks, newer_ref = [ref[...] for ref in refs[:-1]], refs[-1]
    bents = [jnp.tanh(nn(mixed_ref[...], block)) for block in blocks]
    total, slopes = 0.0, 0.0
    for bent, block in zip(bents, blocks):
        total += nt(bent.astype(BF), block)
        slopes += 1.0 - bent * bent
    pulled = nt(total.astype(BF), whiten_ref[...])
    slope = jnp.sum(slopes, axis=1, keepdims=True)
    newer_ref[...] = (pulled - slope * weights_ref[...]) * scale


def white_kernel(whiten_ref, *refs):
    for k, block in enumerate(refs[:-1]):
        refs[-1][k] = nn(whiten_ref[...], block[...]).astype(BF)


def decor_kernel(last, scale, *refs):
    mine, mates, white_ref = refs[:4], refs[4:8], refs[8]
    outs, scratch = (refs[9:11], refs[11:]) if last else (refs[9:10], refs[10:])
    newer, lower, *held = scratch
    count = mine[0].shape[0]
    low, ax, ay = place()
    chunks = white_ref.shape[0] // 2 if last else white_ref.shape[0]
    for k in range(4):
        spot = 4 * other(ax, k & 2) + other(ay, k & 1)
        for ref, core in ((mine[k], low), (mates[k], 1 - low)):
            start = pl.multiple_of((spot + 2 * core) * count, count)
            newer[pl.ds(start, count), :] = ref[...]
            lower[pl.ds(start, count), :] = ref[...].astype(BF)

    raw = lower[...]
    gram = nt(raw, raw)
    gscale = jnp.sqrt(jnp.sum(gram * gram, keepdims=True) + 1e-06)
    value = 1.5 * newer[...] - (0.5 / gscale) * nn(gram.astype(BF), raw)
    value = value * lax.rsqrt(gscale)
    raw = value.astype(BF)
    gram = nt(raw, raw).astype(BF)
    newer[...] = 1.5 * value - 0.5 * nn(gram, raw)
    lower[...] = newer[...].astype(BF)
    start = pl.multiple_of((4 * ax + 2 * low) * count, count)
    size = 2 * count
    if not last:
        start = pl.multiple_of(start + ay * count, count)
        size = count
    raw = lower[...]
    gram = nt(lower[pl.ds(start, size), :], raw).astype(BF)
    weights = 1.5 * newer[pl.ds(start, size), :] - 0.5 * nn(gram, raw)
    if last:
        unmixing, sources, sems = held
        unmixing[...] = weights
        copies = [pltpu.make_async_copy(unmixing, outs[0], sems.at[chunks])]
        copies[0].start()
        width = white_ref.shape[2]
        for k in range(chunks):
            sources[k] = nn(weights.astype(BF), white_ref[k]).astype(BF)
            spot = 2 * other(ax, k & 2) + other(low, k & 1)
            spot = pl.ds(pl.multiple_of(spot * width, width), width)
            copies.append(
                pltpu.make_async_copy(sources.at[k], outs[1].at[:, spot], sems.at[k])
            )
            copies[-1].start()
        for copy in copies:
            copy.wait()
    else:
        total, slope = step(weights, [white_ref[k] for k in range(chunks)])
        outs[0][...] = (total - slope * weights) * scale


def shards(data, projection, initial):
    comps = lax.axis_size("comp")
    voxels = data.shape[1] * lax.axis_size("vox")
    all_bits = (lax.axis_size("vox") * comps).bit_length() - 1
    low, across, near = 1, 2, comps
    far = [1 << k for k in range(near.bit_length(), all_bits)]
    core, far_x, near_y = place()
    rows = projection.shape[0]
    size = data.shape[1] // comps

    mate = flip(projection, low)

    def columns(x, core):
        return lax.dynamic_slice_in_dim(data, (x * 2 + core) * size, size, 1)

    sides = (1 - far_x, far_x)
    theirs = [flip(columns(x, 1 - core), low) for x in sides]
    mine = [columns(x, core) for x in sides]
    sent, kept = (
        run(kernel, shape((count, size), F32), (projection, mine[k], mate, theirs[k]))
        for k, (kernel, count) in enumerate(
            ((sent_kernel, rows + 16), (project_kernel, rows))
        )
    )
    sent = flip(sent.astype(HALF), across).astype(F32)
    reduced = (kept + sent[:rows] * jnp.exp2(sent[rows : rows + 1])).astype(BF)

    block = rows // 4
    piece = 5 * block // 4
    small = shape((piece, block), BF)
    there = flip(reduced, low)
    own, by, bx, bxy = run(
        covar_kernel,
        (shape((piece, block), F32), small, small, small),
        (reduced, there),
        scratch=[pltpu.VMEM((5 * block, block), F32)],
    )
    own, reduced = lax.optimization_barrier((own, reduced))
    at_x, at_y = flip(reduced, across), flip(reduced, near)
    own = own + flip(bxy, across | near).astype(F32)
    own = own + flip(bx, across).astype(F32)
    own = own + flip(by, near).astype(F32)
    own, reduced = lax.optimization_barrier((own, reduced))
    at_xy = flip(reduced, across | near)
    packed, at_x, at_y = sum_over(own, far, BF, (at_x, at_y))
    packed, at_xy = spread(packed, across, near, (at_xy,))
    count = initial.shape[0] // 2
    weights = lax.dynamic_slice_in_dim(initial, near_y * count, count, 0)
    whiten, mixed = run(
        functools.partial(whiten_kernel, voxels),
        (shape((rows, rows), BF), shape((count, rows), BF)),
        (*packed, weights),
        scratch=[pltpu.VMEM((2, 5 * block, block), F32), pltpu.VMEM((rows, rows), F32)],
    )

    scale = 8192.0 / voxels
    blocks = (reduced, there, at_x, flip(at_x, low))
    blocks += (at_y, flip(at_y, low), at_xy, flip(at_xy, low))
    newer = run(
        functools.partial(apply_kernel, scale),
        shape((count, rows), F32),
        (mixed, whiten, weights, *blocks),
    )
    newer, whiten = lax.optimization_barrier((newer, whiten))

    for turn in range(ICA_ITERS):
        last = turn == ICA_ITERS - 1
        if not turn:
            white = run(
                white_kernel,
                shape((len(blocks), rows, size), BF),
                (whiten, *blocks),
                cost=2 * len(blocks) * rows * rows * size,
            )
        (summed, *held) = sum_over(newer, far, HALF, () if turn else (white,))
        if held:
            (white,) = held
        stacked = spread(summed, across, near)
        stacked = [part.astype(F32) * (1.0 / scale) for part in stacked]
        chunks = len(blocks) // 2 if last else len(blocks)
        outs = (
            (shape((2 * count, rows), F32), shape((2 * count, data.shape[1]), BF))
            if last
            else shape((count, rows), F32)
        )
        scratch = [
            pltpu.VMEM((rows, rows), F32),
            pltpu.VMEM((rows, rows), BF),
        ]
        if last:
            scratch += [
                pltpu.VMEM((2 * count, rows), F32),
                pltpu.VMEM((chunks, 2 * count, size), BF),
                pltpu.SemaphoreType.DMA((chunks + 1,)),
            ]
        newer = run(
            functools.partial(decor_kernel, last, scale),
            outs,
            (*stacked, white),
            out_spec=HBM if last else VMEM,
            scratch=scratch,
        )
    return newer


def solution(mesh):
    return jax.shard_map(
        shards,
        mesh=mesh,
        in_specs=(P("comp", "vox"), P(None, "comp"), P("comp", None)),
        out_specs=(P("comp", None), P("comp", "vox")),
        check_vma=False,
    )
```

```python
import functools

import jax
import jax.numpy as jnp
from jax import lax
from jax.experimental import pallas as pl
from jax.experimental.pallas import tpu as pltpu
from jax.sharding import PartitionSpec as P

ICA_ITERS = 2
AXES = ("vox", "comp")
BF = jnp.bfloat16
HALF = jnp.float16
F32 = jnp.float32
MIB = 1 << 20


def place():
    vox, comp = lax.axis_index("vox"), lax.axis_index("comp")
    return lax.rem(comp, 2), lax.div(comp, 2), lax.rem(vox, 2)


def other(bit, flipped):
    return 1 - bit if flipped else bit


def nn(left, right):
    return jnp.dot(left, right, preferred_element_type=F32)


def nt(left, right):
    return lax.dot_general(
        left, right, (((1,), (1,)), ((), ())), preferred_element_type=F32
    )


def rounded(x, kind):
    info = jnp.finfo(kind)
    return lax.reduce_precision(x, info.nexp, info.nmant)


def flip(x, mask):
    count = lax.axis_size("vox") * lax.axis_size("comp")
    return lax.ppermute(x, AXES, [(i, i ^ mask) for i in range(count)])


def sum_over(x, masks, kind, due=()):
    for k in range(0, len(masks), 2):
        sent = x.astype(kind)
        x = rounded(x, kind) + flip(sent, masks[k]).astype(F32)
        if k + 1 < len(masks):
            both = flip(sent, masks[k] | masks[k + 1])
            if k == 0:
                both, *due = lax.optimization_barrier((both, *due))
            x = x + (flip(sent, masks[k + 1]).astype(F32) + both.astype(F32))
    return (x.astype(kind), *due)


def spread(x, across, near, due=()):
    both = flip(x, across | near)
    both, *due = lax.optimization_barrier((both, *due))
    blocks = [x, flip(x, near), flip(x, across), both]
    if due:
        mates = flip(jnp.stack(blocks), 1)
        return (blocks + [mates[k] for k in range(4)], *due)
    return blocks + [flip(block, 1) for block in blocks]


VMEM = pl.BlockSpec(memory_space=pltpu.VMEM)
HBM = pl.BlockSpec(memory_space=pltpu.HBM)


def run(kernel, outs, args, specs=None, out_spec=VMEM, scratch=(), cost=0):
    return pl.pallas_call(
        kernel,
        out_shape=outs,
        in_specs=specs or [VMEM] * len(args),
        out_specs=jax.tree.map(lambda _: out_spec, outs),
        scratch_shapes=list(scratch),
        compiler_params=pltpu.CompilerParams(vmem_limit_bytes=24 * MIB),
        cost_estimate=pl.CostEstimate(flops=cost, bytes_accessed=cost // 256, transcendentals=0)
        if cost
        else None,
    )(*args)


def shape(dims, dtype):
    return jax.ShapeDtypeStruct(dims, dtype)


def sent_kernel(left_ref, right_ref, mate_left_ref, mate_right_ref, out_ref):
    total = nn(left_ref[...], right_ref[...])
    total += nn(mate_left_ref[...], mate_right_ref[...])
    rows = total.shape[0]
    most = jnp.max(jnp.abs(total), axis=0, keepdims=True)
    power = jnp.floor(jnp.log2(jnp.maximum(most, 1e-30))) - 14.0
    out_ref[:rows] = total * jnp.exp2(-power)
    out_ref[rows:] = jnp.broadcast_to(power, (out_ref.shape[0] - rows, total.shape[1]))


def project_kernel(left_ref, right_ref, mate_left_ref, mate_right_ref, out_ref):
    total = nn(left_ref[...], right_ref[...])
    total += nn(mate_left_ref[...], mate_right_ref[...])
    out_ref[...] = total.astype(out_ref.dtype)


def covar_kernel(here_ref, there_ref, own_ref, y_ref, x_ref, xy_ref, pack):
    rows = here_ref.shape[0]
    block = rows // 4

    def product(i, j, count):
        total = 0.0
        for ref in (here_ref, there_ref):
            left = ref[pl.ds(pl.multiple_of(i * block, block), count * block), :]
            right = ref[pl.ds(pl.multiple_of(j * block, block), 2 * block), :]
            total += nt(left, right)
        return total

    low, ax, ay = place()
    corner = product(2 * low, 2 * low, 2)
    cross = product(2 + low, 0, 1)
    pack[0 * block : 1 * block] = corner[:block, :block]
    pack[1 * block : 2 * block] = corner[:block, block:]
    pack[2 * block : 3 * block] = corner[block:, block:]
    pack[3 * block : 4 * block] = cross[:, :block]
    pack[4 * block : 5 * block] = cross[:, block:]
    piece = own_ref.shape[0]

    def quarter(i, j):
        return pack[pl.ds(pl.multiple_of((2 * i + j) * piece, piece), piece), :]

    own_ref[...] = quarter(ax, ay)
    y_ref[...] = quarter(ax, 1 - ay).astype(BF)
    x_ref[...] = quarter(1 - ax, ay).astype(BF)
    xy_ref[...] = quarter(1 - ax, 1 - ay).astype(BF)


def whiten_kernel(voxels, *refs):
    mine, mates = refs[:4], refs[4:8]
    weights_ref, out_ref, mixed_ref, packs, covar = refs[8:]
    piece, block = mine[0].shape
    rows = covar.shape[0]
    low, ax, ay = place()
    for k in range(4):
        spot = 2 * other(ax, k & 1) + other(ay, k & 2)
        spot = pl.ds(pl.multiple_of(spot * piece, piece), piece)
        packs[low, spot, :] = mine[k][...].astype(F32) * (1.0 / voxels)
        packs[1 - low, spot, :] = mates[k][...].astype(F32) * (1.0 / voxels)

    squares = jnp.zeros((block, block), F32)

    def put(i, j, core, k):
        value = packs[core, k * block : (k + 1) * block, :]
        covar[i * block : (i + 1) * block, j * block : (j + 1) * block] = value
        if i == j:
            return value * value
        covar[j * block : (j + 1) * block, i * block : (i + 1) * block] = value.T
        return 2.0 * (value * value)

    for core in (0, 1):
        squares += put(2 * core, 2 * core, core, 0)
        squares += put(2 * core, 2 * core + 1, core, 1)
        squares += put(2 * core + 1, 2 * core + 1, core, 2)
        squares += put(2 + core, 0, core, 3)
        squares += put(2 + core, 1, core, 4)

    cscale = jnp.sqrt(jnp.sum(squares, keepdims=True) + 1e-06)
    y = covar[...] * (1.0 / cscale)
    eye = (
        lax.broadcasted_iota(jnp.int32, (rows, rows), 0)
        == lax.broadcasted_iota(jnp.int32, (rows, rows), 1)
    ).astype(F32)
    yb = y.astype(BF)
    square = nn(yb, yb)
    squared = square.astype(BF)
    rest = -2.4375 * y + 1.6875 * square
    rest += nn(squared, (0.0625 * square - 0.5625 * y).astype(BF))
    restb = rest.astype(BF)
    left = 2.25 * y + nn(yb, restb)
    right = 4.5 * rest + nn(restb, restb)
    z3 = 3.375 * eye + 1.5 * rest - 0.5 * (
        5.0625 * left + nn(left.astype(BF), right.astype(BF))
    )
    whiten = (z3 * lax.rsqrt(cscale)).astype(BF)
    out_ref[...] = whiten
    mixed_ref[...] = nn(weights_ref[...].astype(BF), whiten).astype(BF)


def step(weights, white_ref, turned_ref):
    low = weights.astype(BF)
    total, slopes = 0.0, 0.0
    bents = [jnp.tanh(nn(low, white_ref[k])) for k in range(white_ref.shape[0])]
    for k, bent in enumerate(bents):
        total += nn(bent.astype(BF), turned_ref[k])
        slopes += 1.0 - bent * bent
    return total, jnp.sum(slopes, axis=1, keepdims=True)


def apply_kernel(scale, mixed_ref, whiten_ref, weights_ref, *refs):
    blocks, newer_ref = [ref[...] for ref in refs[:-1]], refs[-1]
    bents = [jnp.tanh(nn(mixed_ref[...], block)) for block in blocks]
    total, slopes = 0.0, 0.0
    for bent, block in zip(bents, blocks):
        total += nt(bent.astype(BF), block)
        slopes += 1.0 - bent * bent
    pulled = nt(total.astype(BF), whiten_ref[...])
    slope = jnp.sum(slopes, axis=1, keepdims=True)
    newer_ref[...] = (pulled - slope * weights_ref[...]) * scale


def white_kernel(whiten_ref, *refs):
    blocks, (white_ref, turned_ref) = refs[:-2], refs[-2:]
    for k, block in enumerate(blocks):
        white = nn(whiten_ref[...], block[...])
        white_ref[k] = white.astype(BF)
        turned_ref[k] = white.astype(BF).T


def decor_kernel(last, scale, *refs):
    mine, mates, white_ref, turned_ref = refs[:4], refs[4:8], refs[8], refs[9]
    outs, scratch = (refs[10:12], refs[12:]) if last else (refs[10:11], refs[11:])
    newer, lower, *held = scratch
    count = mine[0].shape[0]
    low, ax, ay = place()
    chunks = white_ref.shape[0] // 2 if last else white_ref.shape[0]
    for k in range(4):
        spot = 4 * other(ax, k in (1, 2)) + other(ay, k in (1, 3))
        for ref, core in ((mine[k], low), (mates[k], 1 - low)):
            start = pl.multiple_of((spot + 2 * core) * count, count)
            newer[pl.ds(start, count), :] = ref[...]
            lower[pl.ds(start, count), :] = ref[...].astype(BF)

    raw = lower[...]
    gram = nt(raw, raw)
    gscale = jnp.sqrt(jnp.sum(gram * gram, keepdims=True) + 1e-06)
    value = 1.5 * newer[...] - (0.5 / gscale) * nn(gram.astype(BF), raw)
    value = value * lax.rsqrt(gscale)
    raw = value.astype(BF)
    gram = nt(raw, raw).astype(BF)
    newer[...] = 1.5 * value - 0.5 * nn(gram, raw)
    lower[...] = newer[...].astype(BF)
    start = pl.multiple_of((4 * ax + 2 * low) * count, count)
    size = 2 * count
    if not last:
        start = pl.multiple_of(start + ay * count, count)
        size = count
    raw = lower[...]
    gram = nt(lower[pl.ds(start, size), :], raw).astype(BF)
    weights = 1.5 * newer[pl.ds(start, size), :] - 0.5 * nn(gram, raw)
    if last:
        unmixing, sources, sems = held
        unmixing[...] = weights
        copies = [pltpu.make_async_copy(unmixing, outs[0], sems.at[chunks])]
        copies[0].start()
        width = white_ref.shape[2]
        for k in range(chunks):
            sources[k] = nn(weights.astype(BF), white_ref[k]).astype(BF)
            spot = 2 * other(ax, k & 2) + other(low, k & 1)
            spot = pl.ds(pl.multiple_of(spot * width, width), width)
            copies.append(
                pltpu.make_async_copy(sources.at[k], outs[1].at[:, spot], sems.at[k])
            )
            copies[-1].start()
        for copy in copies:
            copy.wait()
    else:
        total, slope = step(weights, white_ref, turned_ref)
        outs[0][...] = (total - slope * weights) * scale


def shards(data, projection, initial):
    comps = lax.axis_size("comp")
    voxels = data.shape[1] * lax.axis_size("vox")
    all_bits = (lax.axis_size("vox") * comps).bit_length() - 1
    low, across, near = 1, 2, comps
    far = [1 << k for k in range(near.bit_length(), all_bits)]
    far = far[1::-1] + far[2:]
    core, far_x, near_y = place()
    rows = projection.shape[0]
    size = data.shape[1] // comps

    mate = flip(projection, low)

    def columns(x, core):
        return lax.dynamic_slice_in_dim(data, (x * 2 + core) * size, size, 1)

    sides = (1 - far_x, far_x)
    theirs = [flip(columns(x, 1 - core), low) for x in sides]
    mine = [columns(x, core) for x in sides]
    sent, kept = (
        run(kernel, shape((count, size), F32), (projection, mine[k], mate, theirs[k]))
        for k, (kernel, count) in enumerate(
            ((sent_kernel, rows + 16), (project_kernel, rows))
        )
    )
    sent = flip(sent.astype(HALF), across).astype(F32)
    reduced = (kept + sent[:rows] * jnp.exp2(sent[rows : rows + 1])).astype(BF)

    block = rows // 4
    piece = 5 * block // 4
    small = shape((piece, block), BF)
    there = flip(reduced, low)
    own, by, bx, bxy = run(
        covar_kernel,
        (shape((piece, block), F32), small, small, small),
        (reduced, there),
        scratch=[pltpu.VMEM((5 * block, block), F32)],
    )
    own, reduced = lax.optimization_barrier((own, reduced))
    at_x, at_y = flip(reduced, across), flip(reduced, near)
    own = own + flip(bxy, across | near).astype(F32)
    own = own + flip(bx, across).astype(F32)
    own = own + flip(by, near).astype(F32)
    own, reduced = lax.optimization_barrier((own, reduced))
    at_xy = flip(reduced, across | near)
    packed, at_y, at_x = sum_over(own, far, BF, (at_y, at_x))
    packed, at_xy = spread(packed, near, across, (at_xy,))
    count = initial.shape[0] // 2
    weights = lax.dynamic_slice_in_dim(initial, near_y * count, count, 0)
    whiten, mixed = run(
        functools.partial(whiten_kernel, voxels),
        (shape((rows, rows), BF), shape((count, rows), BF)),
        (*packed, weights),
        scratch=[pltpu.VMEM((2, 5 * block, block), F32), pltpu.VMEM((rows, rows), F32)],
    )

    scale = 8192.0 / voxels
    blocks = (reduced, there, at_x, flip(at_x, low))
    blocks += (at_y, flip(at_y, low), at_xy, flip(at_xy, low))
    newer = run(
        functools.partial(apply_kernel, scale),
        shape((count, rows), F32),
        (mixed, whiten, weights, *blocks),
    )
    newer, whiten = lax.optimization_barrier((newer, whiten))

    for turn in range(ICA_ITERS):
        last = turn == ICA_ITERS - 1
        if not turn:
            whites = run(
                white_kernel,
                (
                    shape((len(blocks), rows, size), BF),
                    shape((len(blocks), size, rows), BF),
                ),
                (whiten, *blocks),
                cost=2 * len(blocks) * rows * rows * size,
            )
        (summed, *held) = sum_over(newer, far, HALF, () if turn else whites[:1])
        if held:
            whites = (*held, whites[1])
        stacked = spread(summed, across, near)
        stacked = [stacked[k] for k in (0, 3, 2, 1, 4, 7, 6, 5)]
        stacked = [part.astype(F32) * (1.0 / scale) for part in stacked]
        chunks = len(blocks) // 2 if last else len(blocks)
        outs = (
            (shape((2 * count, rows), F32), shape((2 * count, data.shape[1]), BF))
            if last
            else shape((count, rows), F32)
        )
        scratch = [
            pltpu.VMEM((rows, rows), F32),
            pltpu.VMEM((rows, rows), BF),
        ]
        if last:
            scratch += [
                pltpu.VMEM((2 * count, rows), F32),
                pltpu.VMEM((chunks, 2 * count, size), BF),
                pltpu.SemaphoreType.DMA((chunks + 1,)),
            ]
        newer = run(
            functools.partial(decor_kernel, last, scale),
            outs,
            (*stacked, *whites),
            out_spec=HBM if last else VMEM,
            scratch=scratch,
        )
    return newer


def solution(mesh):
    return jax.shard_map(
        shards,
        mesh=mesh,
        in_specs=(P("comp", "vox"), P(None, "comp"), P("comp", None)),
        out_specs=(P("comp", None), P("comp", "vox")),
        check_vma=False,
    )
```

```python
import functools

import jax
import jax.numpy as jnp
from jax import lax
from jax.experimental import pallas as pl
from jax.experimental.pallas import tpu as pltpu
from jax.sharding import PartitionSpec as P

ICA_ITERS = 2
AXES = ("vox", "comp")
BF = jnp.bfloat16
HALF = jnp.float16
F32 = jnp.float32
MIB = 1 << 20


def place():
    vox, comp = lax.axis_index("vox"), lax.axis_index("comp")
    return lax.rem(comp, 2), lax.div(comp, 2), lax.rem(vox, 2)


def other(bit, flipped):
    return 1 - bit if flipped else bit


def nn(left, right):
    return jnp.dot(left, right, preferred_element_type=F32)


def nt(left, right):
    return lax.dot_general(
        left, right, (((1,), (1,)), ((), ())), preferred_element_type=F32
    )


def rounded(x, kind):
    info = jnp.finfo(kind)
    return lax.reduce_precision(x, info.nexp, info.nmant)


def flip(x, mask):
    count = lax.axis_size("vox") * lax.axis_size("comp")
    return lax.ppermute(x, AXES, [(i, i ^ mask) for i in range(count)])


def sum_over(x, masks, kind, due=()):
    for k in range(0, len(masks), 2):
        sent = x.astype(kind)
        x = rounded(x, kind) + flip(sent, masks[k]).astype(F32)
        if k + 1 < len(masks):
            both = flip(sent, masks[k] | masks[k + 1])
            if k == 0:
                both, *due = lax.optimization_barrier((both, *due))
            x = x + (flip(sent, masks[k + 1]).astype(F32) + both.astype(F32))
    return (x.astype(kind), *due)


def spread(x, across, near, due=()):
    both = flip(x, across | near)
    both, *due = lax.optimization_barrier((both, *due))
    blocks = [x, flip(x, near), flip(x, across), both]
    if due:
        mates = flip(jnp.stack(blocks), 1)
        return (blocks + [mates[k] for k in range(4)], *due)
    return blocks + [flip(block, 1) for block in blocks]


VMEM = pl.BlockSpec(memory_space=pltpu.VMEM)
HBM = pl.BlockSpec(memory_space=pltpu.HBM)


def run(kernel, outs, args, specs=None, out_spec=VMEM, scratch=(), cost=0):
    return pl.pallas_call(
        kernel,
        out_shape=outs,
        in_specs=specs or [VMEM] * len(args),
        out_specs=jax.tree.map(lambda _: out_spec, outs),
        scratch_shapes=list(scratch),
        compiler_params=pltpu.CompilerParams(vmem_limit_bytes=24 * MIB),
        cost_estimate=pl.CostEstimate(flops=cost, bytes_accessed=cost // 256, transcendentals=0)
        if cost
        else None,
    )(*args)


def shape(dims, dtype):
    return jax.ShapeDtypeStruct(dims, dtype)


def sent_kernel(left_ref, right_ref, mate_left_ref, mate_right_ref, out_ref):
    total = nn(left_ref[...], right_ref[...])
    total += nn(mate_left_ref[...], mate_right_ref[...])
    rows = total.shape[0]
    most = jnp.max(jnp.abs(total), axis=0, keepdims=True)
    power = jnp.floor(jnp.log2(jnp.maximum(most, 1e-30))) - 14.0
    out_ref[:rows] = total * jnp.exp2(-power)
    out_ref[rows:] = jnp.broadcast_to(power, (out_ref.shape[0] - rows, total.shape[1]))


def project_kernel(left_ref, right_ref, mate_left_ref, mate_right_ref, out_ref):
    total = nn(left_ref[...], right_ref[...])
    total += nn(mate_left_ref[...], mate_right_ref[...])
    out_ref[...] = total.astype(out_ref.dtype)


def covar_kernel(here_ref, there_ref, own_ref, y_ref, x_ref, xy_ref, pack):
    rows = here_ref.shape[0]
    block = rows // 4

    def product(i, j, count):
        total = 0.0
        for ref in (here_ref, there_ref):
            left = ref[pl.ds(pl.multiple_of(i * block, block), count * block), :]
            right = ref[pl.ds(pl.multiple_of(j * block, block), 2 * block), :]
            total += nt(left, right)
        return total

    low, ax, ay = place()
    corner = product(2 * low, 2 * low, 2)
    cross = product(2 + low, 0, 1)
    pack[0 * block : 1 * block] = corner[:block, :block]
    pack[1 * block : 2 * block] = corner[:block, block:]
    pack[2 * block : 3 * block] = corner[block:, block:]
    pack[3 * block : 4 * block] = cross[:, :block]
    pack[4 * block : 5 * block] = cross[:, block:]
    piece = own_ref.shape[0]

    def quarter(i, j):
        return pack[pl.ds(pl.multiple_of((2 * i + j) * piece, piece), piece), :]

    own_ref[...] = quarter(ax, ay)
    y_ref[...] = quarter(ax, 1 - ay).astype(BF)
    x_ref[...] = quarter(1 - ax, ay).astype(BF)
    xy_ref[...] = quarter(1 - ax, 1 - ay).astype(BF)


def whiten_kernel(voxels, *refs):
    mine, mates = refs[:4], refs[4:8]
    weights_ref, out_ref, mixed_ref, packs, covar = refs[8:]
    piece, block = mine[0].shape
    rows = covar.shape[0]
    low, ax, ay = place()
    for k in range(4):
        spot = 2 * other(ax, k & 1) + other(ay, k & 2)
        spot = pl.ds(pl.multiple_of(spot * piece, piece), piece)
        packs[low, spot, :] = mine[k][...].astype(F32) * (1.0 / voxels)
        packs[1 - low, spot, :] = mates[k][...].astype(F32) * (1.0 / voxels)

    squares = jnp.zeros((block, block), F32)

    def put(i, j, core, k):
        value = packs[core, k * block : (k + 1) * block, :]
        covar[i * block : (i + 1) * block, j * block : (j + 1) * block] = value
        if i == j:
            return value * value
        covar[j * block : (j + 1) * block, i * block : (i + 1) * block] = value.T
        return 2.0 * (value * value)

    for core in (0, 1):
        squares += put(2 * core, 2 * core, core, 0)
        squares += put(2 * core, 2 * core + 1, core, 1)
        squares += put(2 * core + 1, 2 * core + 1, core, 2)
        squares += put(2 + core, 0, core, 3)
        squares += put(2 + core, 1, core, 4)

    cscale = jnp.sqrt(jnp.sum(squares, keepdims=True) + 1e-06)
    y = covar[...] * (1.0 / cscale)
    eye = (
        lax.broadcasted_iota(jnp.int32, (rows, rows), 0)
        == lax.broadcasted_iota(jnp.int32, (rows, rows), 1)
    ).astype(F32)
    yb = y.astype(BF)
    parts = [slice(k, k + rows // 2) for k in (0, rows // 2)]

    def product(left, right):
        return [nn(part, right) for part in left]

    def whole(halves):
        return jnp.concatenate([half.astype(BF) for half in halves])

    ys, ybs = [y[part] for part in parts], [yb[part] for part in parts]
    squares = product(ybs, yb)
    inner = whole([0.0625 * s - 0.5625 * part for s, part in zip(squares, ys)])
    thirds = product([s.astype(BF) for s in squares], inner)
    rest = [
        -2.4375 * part + 1.6875 * s + third
        for part, s, third in zip(ys, squares, thirds)
    ]
    restb = whole(rest)
    rights = product([half.astype(BF) for half in rest], restb)
    right = whole([4.5 * half + more for half, more in zip(rest, rights)])
    lefts = [2.25 * part + more for part, more in zip(ys, product(ybs, restb))]
    lasts = product([left.astype(BF) for left in lefts], right)
    for part, half, left, more in zip(parts, rest, lefts, lasts):
        z3 = 3.375 * eye[part] + 1.5 * half - 0.5 * (5.0625 * left + more)
        out_ref[part] = (z3 * lax.rsqrt(cscale)).astype(BF)
    whiten = out_ref[...]
    mixed_ref[...] = nn(weights_ref[...].astype(BF), whiten).astype(BF)


def step(weights, white_ref, turned_ref):
    low = weights.astype(BF)
    total, slopes = 0.0, 0.0
    bents = [jnp.tanh(nn(low, white_ref[k])) for k in range(white_ref.shape[0])]
    for k, bent in enumerate(bents):
        total += nn(bent.astype(BF), turned_ref[k])
        slopes += 1.0 - bent * bent
    return total, jnp.sum(slopes, axis=1, keepdims=True)


def apply_kernel(scale, mixed_ref, whiten_ref, weights_ref, *refs):
    blocks, newer_ref = [ref[...] for ref in refs[:-1]], refs[-1]
    bents = [jnp.tanh(nn(mixed_ref[...], block)) for block in blocks]
    total, slopes = 0.0, 0.0
    for bent, block in zip(bents, blocks):
        total += nt(bent.astype(BF), block)
        slopes += 1.0 - bent * bent
    pulled = nt(total.astype(BF), whiten_ref[...])
    slope = jnp.sum(slopes, axis=1, keepdims=True)
    newer_ref[...] = (pulled - slope * weights_ref[...]) * scale


def white_kernel(whiten_ref, *refs):
    blocks, (white_ref, turned_ref) = refs[:-2], refs[-2:]
    for k, block in enumerate(blocks):
        white = nn(whiten_ref[...], block[...])
        white_ref[k] = white.astype(BF)
        turned_ref[k] = white.astype(BF).T


def decor_kernel(last, scale, *refs):
    mine, mates, white_ref, turned_ref = refs[:4], refs[4:8], refs[8], refs[9]
    outs, scratch = (refs[10:12], refs[12:]) if last else (refs[10:11], refs[11:])
    newer, lower, *held = scratch
    count = mine[0].shape[0]
    low, ax, ay = place()
    chunks = white_ref.shape[0] // 2 if last else white_ref.shape[0]
    for k in range(4):
        spot = 4 * other(ax, k in (1, 2)) + other(ay, k in (1, 3))
        for ref, core in ((mine[k], low), (mates[k], 1 - low)):
            start = pl.multiple_of((spot + 2 * core) * count, count)
            newer[pl.ds(start, count), :] = ref[...]
            lower[pl.ds(start, count), :] = ref[...].astype(BF)

    raw = lower[...]
    rows = raw.shape[0]
    half = rows // 2
    halves = (slice(0, half), slice(half, rows))
    grams = [nt(raw[part], raw) for part in halves]
    squares = sum(jnp.sum(gram * gram, keepdims=True) for gram in grams)
    gscale = jnp.sqrt(squares + 1e-06)
    factor, root = 0.5 / gscale, lax.rsqrt(gscale)
    values = [
        (1.5 * newer[part] - factor * nn(gram.astype(BF), raw)) * root
        for part, gram in zip(halves, grams)
    ]
    raw = jnp.concatenate([value.astype(BF) for value in values])
    for part, value in zip(halves, values):
        gram = nt(raw[part], raw).astype(BF)
        value = 1.5 * value - 0.5 * nn(gram, raw)
        newer[part] = value
        lower[part] = value.astype(BF)
    start = pl.multiple_of((4 * ax + 2 * low) * count, count)
    size = 2 * count
    if not last:
        start = pl.multiple_of(start + ay * count, count)
        size = count
    raw = lower[...]
    gram = nt(lower[pl.ds(start, size), :], raw).astype(BF)
    weights = 1.5 * newer[pl.ds(start, size), :] - 0.5 * nn(gram, raw)
    if last:
        unmixing, sources, sems = held
        unmixing[...] = weights
        copies = [pltpu.make_async_copy(unmixing, outs[0], sems.at[chunks])]
        copies[0].start()
        width = white_ref.shape[2]
        for k in range(chunks):
            sources[k] = nn(weights.astype(BF), white_ref[k]).astype(BF)
            spot = 2 * other(ax, k & 2) + other(low, k & 1)
            spot = pl.ds(pl.multiple_of(spot * width, width), width)
            copies.append(
                pltpu.make_async_copy(sources.at[k], outs[1].at[:, spot], sems.at[k])
            )
            copies[-1].start()
        for copy in copies:
            copy.wait()
    else:
        total, slope = step(weights, white_ref, turned_ref)
        outs[0][...] = (total - slope * weights) * scale


def shards(data, projection, initial):
    comps = lax.axis_size("comp")
    voxels = data.shape[1] * lax.axis_size("vox")
    all_bits = (lax.axis_size("vox") * comps).bit_length() - 1
    low, across, near = 1, 2, comps
    far = [1 << k for k in range(near.bit_length(), all_bits)]
    far = far[1::-1] + far[2:]
    core, far_x, near_y = place()
    rows = projection.shape[0]
    size = data.shape[1] // comps

    mate = flip(projection, low)

    def columns(x, core):
        return lax.dynamic_slice_in_dim(data, (x * 2 + core) * size, size, 1)

    sides = (1 - far_x, far_x)
    theirs = [flip(columns(x, 1 - core), low) for x in sides]
    mine = [columns(x, core) for x in sides]
    sent, kept = (
        run(kernel, shape((count, size), F32), (projection, mine[k], mate, theirs[k]))
        for k, (kernel, count) in enumerate(
            ((sent_kernel, rows + 16), (project_kernel, rows))
        )
    )
    sent = flip(sent.astype(HALF), across).astype(F32)
    reduced = (kept + sent[:rows] * jnp.exp2(sent[rows : rows + 1])).astype(BF)

    block = rows // 4
    piece = 5 * block // 4
    small = shape((piece, block), BF)
    there = flip(reduced, low)
    own, by, bx, bxy = run(
        covar_kernel,
        (shape((piece, block), F32), small, small, small),
        (reduced, there),
        scratch=[pltpu.VMEM((5 * block, block), F32)],
    )
    own, reduced = lax.optimization_barrier((own, reduced))
    at_x, at_y = flip(reduced, across), flip(reduced, near)
    own = own + flip(bxy, across | near).astype(F32)
    own = own + flip(bx, across).astype(F32)
    own = own + flip(by, near).astype(F32)
    own, reduced = lax.optimization_barrier((own, reduced))
    at_xy = flip(reduced, across | near)
    packed, at_y, at_x = sum_over(own, far, BF, (at_y, at_x))
    packed, at_xy = spread(packed, near, across, (at_xy,))
    count = initial.shape[0] // 2
    weights = lax.dynamic_slice_in_dim(initial, near_y * count, count, 0)
    whiten, mixed = run(
        functools.partial(whiten_kernel, voxels),
        (shape((rows, rows), BF), shape((count, rows), BF)),
        (*packed, weights),
        scratch=[pltpu.VMEM((2, 5 * block, block), F32), pltpu.VMEM((rows, rows), F32)],
    )

    scale = 8192.0 / voxels
    blocks = (reduced, there, at_x, flip(at_x, low))
    blocks += (at_y, flip(at_y, low), at_xy, flip(at_xy, low))
    newer = run(
        functools.partial(apply_kernel, scale),
        shape((count, rows), F32),
        (mixed, whiten, weights, *blocks),
    )
    newer, whiten = lax.optimization_barrier((newer, whiten))

    for turn in range(ICA_ITERS):
        last = turn == ICA_ITERS - 1
        if not turn:
            whites = run(
                white_kernel,
                (
                    shape((len(blocks), rows, size), BF),
                    shape((len(blocks), size, rows), BF),
                ),
                (whiten, *blocks),
                cost=2 * len(blocks) * rows * rows * size,
            )
        (summed, *held) = sum_over(newer, far, HALF, () if turn else whites[:1])
        if held:
            whites = (*held, whites[1])
        stacked = spread(summed, across, near)
        stacked = [stacked[k] for k in (0, 3, 2, 1, 4, 7, 6, 5)]
        stacked = [part.astype(F32) * (1.0 / scale) for part in stacked]
        chunks = len(blocks) // 2 if last else len(blocks)
        outs = (
            (shape((2 * count, rows), F32), shape((2 * count, data.shape[1]), BF))
            if last
            else shape((count, rows), F32)
        )
        scratch = [
            pltpu.VMEM((rows, rows), F32),
            pltpu.VMEM((rows, rows), BF),
        ]
        if last:
            scratch += [
                pltpu.VMEM((2 * count, rows), F32),
                pltpu.VMEM((chunks, 2 * count, size), BF),
                pltpu.SemaphoreType.DMA((chunks + 1,)),
            ]
        newer = run(
            functools.partial(decor_kernel, last, scale),
            outs,
            (*stacked, *whites),
            out_spec=HBM if last else VMEM,
            scratch=scratch,
        )
    return newer


def solution(mesh):
    return jax.shard_map(
        shards,
        mesh=mesh,
        in_specs=(P("comp", "vox"), P(None, "comp"), P("comp", None)),
        out_specs=(P("comp", None), P("comp", "vox")),
        check_vma=False,
    )
```

```python
import functools

import jax
import jax.numpy as jnp
from jax import lax
from jax.experimental import pallas as pl
from jax.experimental.pallas import tpu as pltpu
from jax.sharding import PartitionSpec as P

ICA_ITERS = 2
AXES = ("vox", "comp")
BF = jnp.bfloat16
HALF = jnp.float16
F32 = jnp.float32
MIB = 1 << 20


def place():
    vox, comp = lax.axis_index("vox"), lax.axis_index("comp")
    return lax.rem(comp, 2), lax.div(comp, 2), lax.rem(vox, 2)


def other(bit, flipped):
    return 1 - bit if flipped else bit


def nn(left, right):
    return jnp.dot(left, right, preferred_element_type=F32)


def nt(left, right):
    return lax.dot_general(
        left, right, (((1,), (1,)), ((), ())), preferred_element_type=F32
    )


def flip(x, mask):
    count = lax.axis_size("vox") * lax.axis_size("comp")
    return lax.ppermute(x, AXES, [(i, i ^ mask) for i in range(count)])


def sum_over(x, masks, kind, due=()):
    for k in range(0, len(masks), 2):
        sent = lax.optimization_barrier(x.astype(kind))
        x = sent.astype(F32) + flip(sent, masks[k]).astype(F32)
        if k + 1 < len(masks):
            both = flip(sent, masks[k] | masks[k + 1])
            if k == 0:
                both, *due = lax.optimization_barrier((both, *due))
            x = x + (flip(sent, masks[k + 1]).astype(F32) + both.astype(F32))
    return (x.astype(kind), *due)


def spread(x, across, near, due=()):
    both = flip(x, across | near)
    both, *due = lax.optimization_barrier((both, *due))
    blocks = [x, flip(x, near), flip(x, across), both]
    if due:
        mates = flip(jnp.stack(blocks), 1)
        return (blocks + [mates[k] for k in range(4)], *due)
    return blocks + [flip(block, 1) for block in blocks]


VMEM = pl.BlockSpec(memory_space=pltpu.VMEM)
HBM = pl.BlockSpec(memory_space=pltpu.HBM)


def run(kernel, outs, args, specs=None, out_spec=VMEM, scratch=(), cost=0):
    return pl.pallas_call(
        kernel,
        out_shape=outs,
        in_specs=specs or [VMEM] * len(args),
        out_specs=jax.tree.map(lambda _: out_spec, outs),
        scratch_shapes=list(scratch),
        compiler_params=pltpu.CompilerParams(vmem_limit_bytes=24 * MIB),
        cost_estimate=pl.CostEstimate(flops=cost, bytes_accessed=cost // 256, transcendentals=0)
        if cost
        else None,
    )(*args)


def shape(dims, dtype):
    return jax.ShapeDtypeStruct(dims, dtype)


def sent_kernel(left_ref, right_ref, mate_left_ref, mate_right_ref, out_ref):
    total = nn(left_ref[...], right_ref[...])
    total += nn(mate_left_ref[...], mate_right_ref[...])
    rows = total.shape[0]
    most = jnp.max(jnp.abs(total), axis=0, keepdims=True)
    power = jnp.floor(jnp.log2(jnp.maximum(most, 1e-30))) - 14.0
    out_ref[:rows] = total * jnp.exp2(-power)
    out_ref[rows:] = jnp.broadcast_to(power, (out_ref.shape[0] - rows, total.shape[1]))


def project_kernel(left_ref, right_ref, mate_left_ref, mate_right_ref, out_ref):
    total = nn(left_ref[...], right_ref[...])
    total += nn(mate_left_ref[...], mate_right_ref[...])
    out_ref[...] = total.astype(out_ref.dtype)


def covar_kernel(here_ref, there_ref, own_ref, y_ref, x_ref, xy_ref, pack):
    rows = here_ref.shape[0]
    block = rows // 4

    def product(i, j, count):
        total = 0.0
        for ref in (here_ref, there_ref):
            left = ref[pl.ds(pl.multiple_of(i * block, block), count * block), :]
            right = ref[pl.ds(pl.multiple_of(j * block, block), 2 * block), :]
            total += nt(left, right)
        return total

    low, ax, ay = place()
    corner = product(2 * low, 2 * low, 2)
    cross = product(2 + low, 0, 1)
    pack[0 * block : 1 * block] = corner[:block, :block]
    pack[1 * block : 2 * block] = corner[:block, block:]
    pack[2 * block : 3 * block] = corner[block:, block:]
    pack[3 * block : 4 * block] = cross[:, :block]
    pack[4 * block : 5 * block] = cross[:, block:]
    piece = own_ref.shape[0]

    def quarter(i, j):
        return pack[pl.ds(pl.multiple_of((2 * i + j) * piece, piece), piece), :]

    own_ref[...] = quarter(ax, ay)
    y_ref[...] = quarter(ax, 1 - ay).astype(BF)
    x_ref[...] = quarter(1 - ax, ay).astype(BF)
    xy_ref[...] = quarter(1 - ax, 1 - ay).astype(BF)


def whiten_kernel(voxels, *refs):
    mine, mates = refs[:4], refs[4:8]
    weights_ref, out_ref, mixed_ref, packs, covar = refs[8:]
    piece, block = mine[0].shape
    rows = covar.shape[0]
    low, ax, ay = place()
    for k in range(4):
        spot = 2 * other(ax, k & 1) + other(ay, k & 2)
        spot = pl.ds(pl.multiple_of(spot * piece, piece), piece)
        packs[low, spot, :] = mine[k][...].astype(F32) * (1.0 / voxels)
        packs[1 - low, spot, :] = mates[k][...].astype(F32) * (1.0 / voxels)

    squares = jnp.zeros((block, block), F32)

    def put(i, j, core, k):
        value = packs[core, k * block : (k + 1) * block, :]
        covar[i * block : (i + 1) * block, j * block : (j + 1) * block] = value
        if i == j:
            return value * value
        covar[j * block : (j + 1) * block, i * block : (i + 1) * block] = value.T
        return 2.0 * (value * value)

    for core in (0, 1):
        squares += put(2 * core, 2 * core, core, 0)
        squares += put(2 * core, 2 * core + 1, core, 1)
        squares += put(2 * core + 1, 2 * core + 1, core, 2)
        squares += put(2 + core, 0, core, 3)
        squares += put(2 + core, 1, core, 4)

    cscale = jnp.sqrt(jnp.sum(squares, keepdims=True) + 1e-06)
    y = covar[...] * (1.0 / cscale)
    eye = (
        lax.broadcasted_iota(jnp.int32, (rows, rows), 0)
        == lax.broadcasted_iota(jnp.int32, (rows, rows), 1)
    ).astype(F32)
    yb = y.astype(BF)
    parts = [slice(k, k + rows // 2) for k in (0, rows // 2)]

    def product(left, right):
        return [nn(part, right) for part in left]

    def whole(halves):
        return jnp.concatenate([half.astype(BF) for half in halves])

    ys, ybs = [y[part] for part in parts], [yb[part] for part in parts]
    squares = product(ybs, yb)
    inner = whole([0.0625 * s - 0.5625 * part for s, part in zip(squares, ys)])
    thirds = product([s.astype(BF) for s in squares], inner)
    rest = [
        -2.4375 * part + 1.6875 * s + third
        for part, s, third in zip(ys, squares, thirds)
    ]
    restb = whole(rest)
    rights = product([half.astype(BF) for half in rest], restb)
    right = whole([4.5 * half + more for half, more in zip(rest, rights)])
    lefts = [2.25 * part + more for part, more in zip(ys, product(ybs, restb))]
    lasts = product([left.astype(BF) for left in lefts], right)
    for part, half, left, more in zip(parts, rest, lefts, lasts):
        z3 = 3.375 * eye[part] + 1.5 * half - 0.5 * (5.0625 * left + more)
        out_ref[part] = (z3 * lax.rsqrt(cscale)).astype(BF)
    whiten = out_ref[...]
    mixed_ref[...] = nn(weights_ref[...].astype(BF), whiten).astype(BF)


def step(weights, white_ref, turned_ref):
    low = weights.astype(BF)
    total, slopes = 0.0, 0.0
    bents = [jnp.tanh(nn(low, white_ref[k])) for k in range(white_ref.shape[0])]
    for k, bent in enumerate(bents):
        total += nn(bent.astype(BF), turned_ref[k])
        slopes += 1.0 - bent * bent
    return total, jnp.sum(slopes, axis=1, keepdims=True)


def apply_kernel(scale, mixed_ref, whiten_ref, weights_ref, *refs):
    blocks, newer_ref = [ref[...] for ref in refs[:-1]], refs[-1]
    bents = [jnp.tanh(nn(mixed_ref[...], block)) for block in blocks]
    total, slopes = 0.0, 0.0
    for bent, block in zip(bents, blocks):
        total += nt(bent.astype(BF), block)
        slopes += 1.0 - bent * bent
    pulled = nt(total.astype(BF), whiten_ref[...])
    slope = jnp.sum(slopes, axis=1, keepdims=True)
    newer_ref[...] = (pulled - slope * weights_ref[...]) * scale


def white_kernel(whiten_ref, *refs):
    blocks, (white_ref, turned_ref) = refs[:-2], refs[-2:]
    for k, block in enumerate(blocks):
        white = nn(whiten_ref[...], block[...])
        white_ref[k] = white.astype(BF)
        turned_ref[k] = white.astype(BF).T


def decor_kernel(last, scale, *refs):
    mine, mates, white_ref, turned_ref = refs[:4], refs[4:8], refs[8], refs[9]
    outs, scratch = (refs[10:12], refs[12:]) if last else (refs[10:11], refs[11:])
    newer, lower, *held = scratch
    count = mine[0].shape[0]
    low, ax, ay = place()
    chunks = white_ref.shape[0] // 2 if last else white_ref.shape[0]
    for k in range(4):
        spot = 4 * other(ax, k in (1, 2)) + other(ay, k in (1, 3))
        for ref, core in ((mine[k], low), (mates[k], 1 - low)):
            start = pl.multiple_of((spot + 2 * core) * count, count)
            newer[pl.ds(start, count), :] = ref[...]
            lower[pl.ds(start, count), :] = ref[...].astype(BF)

    raw = lower[...]
    rows = raw.shape[0]
    half = rows // 2
    halves = (slice(0, half), slice(half, rows))
    grams = [nt(raw[part], raw) for part in halves]
    squares = sum(jnp.sum(gram * gram, keepdims=True) for gram in grams)
    gscale = jnp.sqrt(squares + 1e-06)
    factor, root = 0.5 / gscale, lax.rsqrt(gscale)
    values = [
        (1.5 * newer[part] - factor * nn(gram.astype(BF), raw)) * root
        for part, gram in zip(halves, grams)
    ]
    raw = jnp.concatenate([value.astype(BF) for value in values])
    for part, value in zip(halves, values):
        gram = nt(raw[part], raw).astype(BF)
        value = 1.5 * value - 0.5 * nn(gram, raw)
        newer[part] = value
        lower[part] = value.astype(BF)
    start = pl.multiple_of((4 * ax + 2 * low) * count, count)
    size = 2 * count
    if not last:
        start = pl.multiple_of(start + ay * count, count)
        size = count
    raw = lower[...]
    gram = nt(lower[pl.ds(start, size), :], raw).astype(BF)
    weights = 1.5 * newer[pl.ds(start, size), :] - 0.5 * nn(gram, raw)
    if last:
        unmixing, sources, sems = held
        unmixing[...] = weights
        copies = [pltpu.make_async_copy(unmixing, outs[0], sems.at[chunks])]
        copies[0].start()
        width = white_ref.shape[2]
        for k in range(chunks):
            sources[k] = nn(weights.astype(BF), white_ref[k]).astype(BF)
            spot = 2 * other(ax, k & 2) + other(low, k & 1)
            spot = pl.ds(pl.multiple_of(spot * width, width), width)
            copies.append(
                pltpu.make_async_copy(sources.at[k], outs[1].at[:, spot], sems.at[k])
            )
            copies[-1].start()
        for copy in copies:
            copy.wait()
    else:
        total, slope = step(weights, white_ref, turned_ref)
        outs[0][...] = (total - slope * weights) * scale


def shards(data, projection, initial):
    comps = lax.axis_size("comp")
    voxels = data.shape[1] * lax.axis_size("vox")
    all_bits = (lax.axis_size("vox") * comps).bit_length() - 1
    low, across, near = 1, 2, comps
    far = [1 << k for k in range(near.bit_length(), all_bits)]
    far = far[1::-1] + far[2:]
    core, far_x, near_y = place()
    rows = projection.shape[0]
    size = data.shape[1] // comps

    mate = flip(projection, low)

    def columns(x, core):
        return lax.dynamic_slice_in_dim(data, (x * 2 + core) * size, size, 1)

    sides = (1 - far_x, far_x)
    theirs = [flip(columns(x, 1 - core), low) for x in sides]
    mine = [columns(x, core) for x in sides]
    sent, kept = (
        run(kernel, shape((count, size), F32), (projection, mine[k], mate, theirs[k]))
        for k, (kernel, count) in enumerate(
            ((sent_kernel, rows + 16), (project_kernel, rows))
        )
    )
    sent = flip(sent.astype(HALF), across).astype(F32)
    reduced = (kept + sent[:rows] * jnp.exp2(sent[rows : rows + 1])).astype(BF)

    block = rows // 4
    piece = 5 * block // 4
    small = shape((piece, block), BF)
    there = flip(reduced, low)
    own, by, bx, bxy = run(
        covar_kernel,
        (shape((piece, block), F32), small, small, small),
        (reduced, there),
        scratch=[pltpu.VMEM((5 * block, block), F32)],
    )
    own, reduced = lax.optimization_barrier((own, reduced))
    at_x, at_y = flip(reduced, across), flip(reduced, near)
    own = own + flip(bxy, across | near).astype(F32)
    own = own + flip(bx, across).astype(F32)
    own = own + flip(by, near).astype(F32)
    own, reduced = lax.optimization_barrier((own, reduced))
    at_xy = flip(reduced, across | near)
    packed, at_y, at_x = sum_over(own, far, BF, (at_y, at_x))
    packed, at_xy = spread(packed, near, across, (at_xy,))
    count = initial.shape[0] // 2
    weights = lax.dynamic_slice_in_dim(initial, near_y * count, count, 0)
    whiten, mixed = run(
        functools.partial(whiten_kernel, voxels),
        (shape((rows, rows), BF), shape((count, rows), BF)),
        (*packed, weights),
        scratch=[pltpu.VMEM((2, 5 * block, block), F32), pltpu.VMEM((rows, rows), F32)],
    )

    scale = 8192.0 / voxels
    blocks = (reduced, there, at_x, flip(at_x, low))
    blocks += (at_y, flip(at_y, low), at_xy, flip(at_xy, low))
    newer = run(
        functools.partial(apply_kernel, scale),
        shape((count, rows), F32),
        (mixed, whiten, weights, *blocks),
    )
    newer, whiten = lax.optimization_barrier((newer, whiten))

    for turn in range(ICA_ITERS):
        last = turn == ICA_ITERS - 1
        if not turn:
            whites = run(
                white_kernel,
                (
                    shape((len(blocks), rows, size), BF),
                    shape((len(blocks), size, rows), BF),
                ),
                (whiten, *blocks),
                cost=2 * len(blocks) * rows * rows * size,
            )
        (summed, *held) = sum_over(newer, far[1::-1] + far[2:], HALF, () if turn else whites[:1])
        if held:
            whites = (*held, whites[1])
        stacked = spread(summed, across, near)
        stacked = [stacked[k] for k in (0, 3, 2, 1, 4, 7, 6, 5)]
        stacked = [part.astype(F32) * (1.0 / scale) for part in stacked]
        chunks = len(blocks) // 2 if last else len(blocks)
        outs = (
            (shape((2 * count, rows), F32), shape((2 * count, data.shape[1]), BF))
            if last
            else shape((count, rows), F32)
        )
        scratch = [
            pltpu.VMEM((rows, rows), F32),
            pltpu.VMEM((rows, rows), BF),
        ]
        if last:
            scratch += [
                pltpu.VMEM((2 * count, rows), F32),
                pltpu.VMEM((chunks, 2 * count, size), BF),
                pltpu.SemaphoreType.DMA((chunks + 1,)),
            ]
        newer = run(
            functools.partial(decor_kernel, last, scale),
            outs,
            (*stacked, *whites),
            out_spec=HBM if last else VMEM,
            scratch=scratch,
        )
    return newer


def solution(mesh):
    return jax.shard_map(
        shards,
        mesh=mesh,
        in_specs=(P("comp", "vox"), P(None, "comp"), P("comp", None)),
        out_specs=(P("comp", None), P("comp", "vox")),
        check_vma=False,
    )
```
